32 devices in a mesh: gx: 4 (over z), gy: 2 (over x), gz: 4 (over y, core).
Axes of the slice: x: 2, y: 2, z: 4, core: 2. Of those that a mesh axis runs over, the one named last changes fastest.
Arguments:
- dual_blocks: bfloat16 [4, 2, 4, 1024, 1024], P('gx', 'gy', 'gz'), may hold values from -1 to 3, as said below
- load_terms: bfloat16 [4, 2, 4, 1024, 128], P('gx', 'gy', 'gz'), may hold values from -6 to 6
- row_order: int32 [4, 2, 4, 1024], P('gx', 'gy', 'gz'), may hold values from 0 to 1023, each once within a row
- mode_rows: bfloat16 [4, 2, 4, 1024, 6], P('gx', 'gy', 'gz'), may hold values from -0.1875 to 0.1875
- mode_count: int32 [4, 2, 4], P('gx', 'gy', 'gz'), may hold values from 0 to 6, as said below
- coarse_inverse: float32 [4, 2, 24, 24], P('gx', 'gy'), may hold values from -1 to 3, as said below
Outputs:
- multipliers: float32 [4, 2, 4, 1024, 128], P('gx', 'gy', 'gz')
- residual: float32 [4, 2, 4, 1024, 128], P('gx', 'gy', 'gz')
The draws below stay inside these ranges and needn't reach their ends.
Inputs may be any that keep to these rules, and one draw needn't show every extreme that they name: `mode_count`: subdomains away from the outer boundary have 6 rigid-body modes; subdomains on the outer boundary have 0 to 6; some subdomain has exactly 6 and some boundary subdomain has none. Each subdomain's row of row_order is a permutation of its 1024 rows. `dual_blocks`: each subdomain's block is symmetric positive definite. `coarse_inverse`: each line's matrix is symmetric positive definite.
All inputs are finite; a program needn't handle non-finite values.
Results may differ from the reference program's by a relative error of at most 0.0082.
Values sent between devices are 32-bit elements; how exact they have to be, the bound alone decides.
A program may use at most 64 MiB of HBM per device.

```python
import math
import jax
import jax.numpy as jnp
from jax import lax

FACE = 128
EDGE = 16
CORNER = 8
M = 1024
LOADS = 128
NMODE = 6
ITERS = 3
SUB_X = 4
SUB_Y = 2
SUB_Z = 4
COARSE = 24


def draw_dual_blocks(key, part):
    sub_total = SUB_X * SUB_Y * SUB_Z

    def draw_one(index_value):
        sub_key = jax.random.fold_in(key, index_value)
        key_noise, key_diag = jax.random.split(sub_key)
        noise_part = jax.random.normal(key_noise, (M, M), jnp.float32)
        diag_vals = jax.random.uniform(key_diag, (M,), jnp.float32, 1.0, 2.0)
        noise_part = noise_part * (0.3 / math.sqrt(M))
        symmetric = (noise_part + noise_part.T) * 0.70710678
        identity = jnp.eye(M, dtype=jnp.float32)
        return (symmetric + identity * diag_vals[None, :]).astype(jnp.bfloat16)
    blocks = lax.map(draw_one, jnp.arange(sub_total, dtype=jnp.int32))
    return blocks.reshape(SUB_X, SUB_Y, SUB_Z, M, M)


def draw_mode_count(key, part):
    keys = jax.random.split(jax.random.fold_in(key, 17), 7)
    pos_x = jnp.arange(SUB_X, dtype=jnp.int32)[:, None, None]
    pos_y = jnp.arange(SUB_Y, dtype=jnp.int32)[None, :, None]
    pos_z = jnp.arange(SUB_Z, dtype=jnp.int32)[None, None, :]
    boundary = (pos_x == 0) | (pos_x == SUB_X - 1) | (pos_y == 0) | (pos_y == SUB_Y - 1) | (pos_z == 0) | (pos_z == SUB_Z - 1)
    coin = jax.random.randint(keys[0], (SUB_X, SUB_Y, SUB_Z), 0, 2)
    fewer = jax.random.randint(keys[1], (SUB_X, SUB_Y, SUB_Z), 0, NMODE)
    counts = jnp.where(boundary & (coin == 1), fewer, NMODE)
    high_x = jax.random.randint(keys[2], (), 0, SUB_X)
    high_y = jax.random.randint(keys[3], (), 0, SUB_Y)
    high_z = jax.random.randint(keys[4], (), 0, SUB_Z)
    low_x = jax.random.randint(keys[5], (), 0, SUB_X)
    low_y = jax.random.randint(keys[6], (), 0, SUB_Y)
    low_z = jnp.where(high_z == 0, SUB_Z - 1, 0)
    counts = jnp.where((pos_x == high_x) & (pos_y == high_y) & (pos_z == high_z), NMODE, counts)
    counts = jnp.where((pos_x == low_x) & (pos_y == low_y) & (pos_z == low_z), 0, counts)
    return counts.astype(jnp.int32)


def draw_coarse_inverse(key, part):
    key_base, key_diag = jax.random.split(jax.random.fold_in(key, 29))
    base_draw = jax.random.normal(key_base, (SUB_X, SUB_Y, COARSE, COARSE), jnp.float32)
    diag_vals = jax.random.uniform(key_diag, (SUB_X, SUB_Y, COARSE), jnp.float32, 0.05, 0.15)
    wishart = jnp.einsum('abij,abkj->abik', base_draw, base_draw) * (0.4 / COARSE)
    identity = jnp.eye(COARSE, dtype=jnp.float32)
    return wishart + identity[None, None] * diag_vals[..., None, :]


def shard_levels(stream_key, dims, pieces, low, largest):
    gain, own = 1.0, jax.random.fold_in(stream_key, 6)
    for dim, parts in pieces:
        draws = jnp.exp(jax.random.uniform(jax.random.fold_in(own, dim), (parts,), jnp.float32, low / len(pieces), largest / len(pieces)))
        gain = gain * jnp.repeat(draws, dims[dim] // parts).reshape([-1 if axis == dim else 1 for axis in range(len(dims))])
    return gain


def noise(key, shape, scale, most, cuts=(), kind=jnp.bfloat16):
    result = jax.random.normal(key, shape, jnp.float32) * scale
    if len(cuts) > 0:
        result = shard_levels(key, shape, cuts, -0.22, 0.18) * result
    return jnp.clip(result, min=-most, max=most).astype(kind)


def setup_inputs(seed: int = 0) -> dict:
    seeds = jax.random.split(jax.random.key(seed), 7)
    return {
        "dual_blocks": draw_dual_blocks(jax.random.fold_in(seeds[6], 71), 0),
        "load_terms": noise(seeds[1], (SUB_X, SUB_Y, SUB_Z, M, LOADS), 1.0, 6.0, ((0, 4), (1, 2), (2, 4))),
        "row_order": jax.vmap(lambda own: jax.random.permutation(own, M))(jax.random.split(seeds[2], SUB_X * SUB_Y * SUB_Z)).reshape((SUB_X, SUB_Y, SUB_Z, M)).astype(jnp.int32),
        "mode_rows": noise(seeds[3], (SUB_X, SUB_Y, SUB_Z, M, NMODE), M ** -0.5, 0.1875, ((0, 4), (1, 2), (2, 4))),
        "mode_count": draw_mode_count(jax.random.fold_in(seeds[6], 71), 0),
        "coarse_inverse": draw_coarse_inverse(jax.random.fold_in(seeds[6], 71), 0),
    }


EIG_LOW = 0.5
EIG_HIGH = 6.0


def slot_table():
    slot_list = []
    begin_row = 0
    for weight_class, width_rows in ((1, FACE), (2, EDGE), (3, CORNER)):
        for sign_one in (-1, 0, 1):
            for sign_two in (-1, 0, 1):
                for sign_three in (-1, 0, 1):
                    if abs(sign_one) + abs(sign_two) + abs(sign_three) == weight_class:
                        slot_list.append(((sign_one, sign_two, sign_three), begin_row, width_rows))
                        begin_row += width_rows
    return slot_list


def partner_rows(packed):
    padded = jnp.pad(packed, ((1, 1), (1, 1), (1, 1), (0, 0), (0, 0)))
    slot_list = slot_table()
    lookup = {}
    for offset, begin_row, width_rows in slot_list:
        lookup[offset] = begin_row
    blocks = []
    for offset, begin_row, width_rows in slot_list:
        other_begin = lookup[(-offset[0], -offset[1], -offset[2])]
        segment = padded[1 + offset[0]:1 + offset[0] + SUB_X, 1 + offset[1]:1 + offset[1] + SUB_Y,
                         1 + offset[2]:1 + offset[2] + SUB_Z, other_begin:other_begin + width_rows]
        blocks.append(segment)
    return jnp.concatenate(blocks, axis=3)


def pack_rows(values, row_order):
    return jnp.take_along_axis(values, row_order[..., None], axis=3)


def apply_operator(dual_blocks, row_order, direction):
    sub_total = SUB_X * SUB_Y * SUB_Z
    flat_dual = dual_blocks.reshape(sub_total, M, M)
    flat_order = row_order.reshape(sub_total, M)
    rounded = lax.optimization_barrier(direction.astype(jnp.bfloat16))
    flat_vectors = rounded.reshape(sub_total, M, direction.shape[-1])

    def multiply(operands):
        dual_one, packing, vector = operands
        packed_block = jnp.take(jnp.take(dual_one, packing, axis=0), packing, axis=1).astype(jnp.float32)
        return jnp.dot(packed_block, vector.astype(jnp.float32), precision=lax.Precision.HIGHEST)

    images = lax.map(multiply, (flat_dual, flat_order, flat_vectors)).reshape(direction.shape)
    return images + partner_rows(images)


def coarse_step(residual, mode_cols, mode_count, coarse_inverse):
    highest = lax.Precision.HIGHEST
    project = jnp.einsum("abcmk,abcmr->abckr", mode_cols, residual, precision=highest)
    offsets = jnp.cumsum(mode_count, axis=2) - mode_count
    compact_pos = jnp.arange(COARSE, dtype=jnp.int32)
    mode_index = jnp.arange(NMODE, dtype=jnp.int32)
    hits = compact_pos[None, None, None, None, :] == offsets[..., None, None] + mode_index[None, None, None, :, None]
    valid = mode_index[None, None, None, :, None] < mode_count[..., None, None]
    select = jnp.where(hits & valid, 1.0, 0.0).astype(jnp.float32)
    compact = jnp.einsum("abckj,abckr->abjr", select, project, precision=highest)
    solved = jnp.einsum("abij,abjr->abir", coarse_inverse, compact, precision=highest)
    amplitude = jnp.einsum("abckj,abjr->abckr", select, solved, precision=highest)
    spread = jnp.einsum("abcmk,abckr->abcmr", mode_cols, amplitude, precision=highest)
    return residual - spread - partner_rows(spread)


def reference(dual_blocks, load_terms, row_order, mode_rows, mode_count, coarse_inverse):
    load_rows = pack_rows(load_terms.astype(jnp.float32), row_order)
    mode_cols = pack_rows(mode_rows.astype(jnp.float32), row_order)
    center_value = 0.5 * (EIG_HIGH + EIG_LOW)
    half_width = 0.5 * (EIG_HIGH - EIG_LOW)
    residual = load_rows + partner_rows(load_rows)
    direction = coarse_step(residual, mode_cols, mode_count, coarse_inverse) / center_value
    multipliers = direction
    rho_prev = half_width / center_value
    residual = residual - apply_operator(dual_blocks, row_order, direction)
    for iteration in range(1, ITERS):
        corrected = coarse_step(residual, mode_cols, mode_count, coarse_inverse)
        rho_now = 1.0 / (2.0 * center_value / half_width - rho_prev)
        direction = (rho_now * rho_prev) * direction + (2.0 * rho_now / half_width) * corrected
        multipliers = multipliers + direction
        residual = residual - apply_operator(dual_blocks, row_order, direction)
        rho_prev = rho_now
    unpacking = jnp.argsort(row_order, axis=-1).astype(jnp.int32)
    return (jnp.take_along_axis(multipliers, unpacking[..., None], axis=3),
            jnp.take_along_axis(residual, unpacking[..., None], axis=3))
```

```python
import functools

import jax
import jax.numpy as jnp
from jax import lax
from jax.experimental import pallas as pl
from jax.experimental.pallas import tpu as pltpu
from jax.sharding import PartitionSpec as P

FACE = 128
EDGE = 16
CORNER = 8
ITERS = 3
EIG_LOW = 0.5
EIG_HIGH = 6.0

MESH = pl.DeviceIdType.MESH
LANES = 128
SUB = 8
F32 = jnp.float32
BF16 = jnp.bfloat16
HIGHEST = lax.Precision.HIGHEST


def slot_table():
    slots = []
    begin = 0
    for weight, width in ((1, FACE), (2, EDGE), (3, CORNER)):
        for a in (-1, 0, 1):
            for b in (-1, 0, 1):
                for c in (-1, 0, 1):
                    if abs(a) + abs(b) + abs(c) == weight:
                        slots.append(((a, b, c), begin, width))
                        begin += width
    return slots


SLOTS = slot_table()
BEGIN = {offset: begin for offset, begin, _ in SLOTS}
LINES = [(a, b) for a in (-1, 0, 1) for b in (-1, 0, 1)]
OWN = 4
BLOCKS = 3 * len(LINES)


def coefficients():
    center = 0.5 * (EIG_HIGH + EIG_LOW)
    half = 0.5 * (EIG_HIGH - EIG_LOW)
    pairs = [(0.0, 1.0 / center)]
    rho = half / center
    for _ in range(1, ITERS):
        following = 1.0 / (2.0 * center / half - rho)
        pairs.append((following * rho, 2.0 * following / half))
        rho = following
    return pairs


def halves(x):
    high = x.astype(BF16)
    low = (x - high.astype(F32)).astype(BF16)
    return jnp.concatenate([high, low], axis=1)


def kernel(shape, dual_ref, load_ref, order_ref, modes_ref, count_ref, inverse_ref,
           mult_out, res_out,
           perm, perm_t, half_packed, packed, image, received, own_modes, far_modes, wide,
           residual, direction, multipliers, modes_t, mode_pad,
           project_out, projects, inverses, select_pad, select_all, coarse,
           send_a, recv_a, send_m, recv_m, send_b, recv_b, send_i, recv_i):
    nx, ny, nz = shape
    ix, iy, iz = lax.axis_index("gx"), lax.axis_index("gy"), lax.axis_index("gz")
    m = dual_ref.shape[0]
    nmode = modes_ref.shape[0]
    csize = inverse_ref.shape[0]
    cwide = inverses.shape[2]
    line_rows = nz * SUB
    barrier = pltpu.get_barrier_semaphore()

    def line_exists(line):
        a, b = line
        return (ix + a >= 0) & (ix + a < nx) & (iy + b >= 0) & (iy + b < ny)

    def slot_exists(offset):
        return line_exists(offset[:2]) & (iz + offset[2] >= 0) & (iz + offset[2] < nz)

    def each_device(line_index, action):
        def step(t, carry):
            if line_index == OWN:
                @pl.when(t != iz)
                def _():
                    action(t)
            else:
                action(t)
            return carry
        lax.fori_loop(0, nz, step, 0, unroll=nz <= 4)

    for index, line in enumerate(LINES):
        @pl.when(line_exists(line))
        def _(index=index, line=line):
            def greet(t):
                pl.semaphore_signal(barrier, inc=1, device_id=(ix + line[0], iy + line[1], t),
                                    device_id_type=MESH)
            each_device(index, greet)

    def slot_copy(source, target, send, recv, number):
        offset, begin, width = SLOTS[number]
        back = (-offset[0], -offset[1], -offset[2])
        return pltpu.make_async_remote_copy(
            src_ref=source.at[pl.ds(begin, width)],
            dst_ref=target.at[pl.ds(BEGIN[back], width)],
            send_sem=send.at[number],
            recv_sem=recv.at[[s[0] for s in SLOTS].index(back)],
            device_id=(ix + offset[0], iy + offset[1], iz + offset[2]),
            device_id_type=MESH)

    def slot_arrival(target, send, recv, number):
        offset, begin, width = SLOTS[number]
        return pltpu.make_async_remote_copy(
            src_ref=target.at[pl.ds(begin, width)],
            dst_ref=target.at[pl.ds(begin, width)],
            send_sem=send.at[number], recv_sem=recv.at[number],
            device_id=(ix + offset[0], iy + offset[1], iz + offset[2]),
            device_id_type=MESH)

    def send_slots(source, target, send, recv, numbers):
        for number in numbers:
            @pl.when(slot_exists(SLOTS[number][0]))
            def _(number=number):
                slot_copy(source, target, send, recv, number).start()

    def wait_slots(source, target, send, recv):
        for number in range(len(SLOTS)):
            @pl.when(slot_exists(SLOTS[number][0]))
            def _(number=number):
                slot_arrival(target, send, recv, number).wait_recv()
                slot_copy(source, target, send, recv, number).wait_send()

    def send_blocks(phase):
        for index, line in enumerate(LINES):
            @pl.when(line_exists(line))
            def _(index=index, line=line):
                def copy(t):
                    pltpu.make_async_remote_copy(
                        src_ref=project_out.at[phase],
                        dst_ref=projects.at[phase, (8 - index) * nz + iz],
                        send_sem=send_b.at[index],
                        recv_sem=recv_b.at[phase, 8 - index],
                        device_id=(ix + line[0], iy + line[1], t),
                        device_id_type=MESH).start()
                each_device(index, copy)

    def wait_blocks(phase):
        for index, line in enumerate(LINES):
            blocks = nz - 1 if index == OWN else nz
            if blocks == 0:
                continue
            @pl.when(line_exists(line))
            def _(index=index, line=line, blocks=blocks):
                span = projects.at[phase, pl.ds(index * nz, blocks)]
                arrival = pltpu.make_async_remote_copy(
                    src_ref=span, dst_ref=span,
                    send_sem=send_b.at[index], recv_sem=recv_b.at[phase, index],
                    device_id=(ix + line[0], iy + line[1], iz), device_id_type=MESH)
                arrival.wait_recv()
                arrival.wait_send()

    def inverse_copy(index):
        line = LINES[index]
        return pltpu.make_async_remote_copy(
            src_ref=inverses.at[OWN], dst_ref=inverses.at[8 - index],
            send_sem=send_i.at[index], recv_sem=recv_i.at[8 - index],
            device_id=(ix + line[0], iy + line[1], iz), device_id_type=MESH)

    def publish(phase, block):
        project_out[phase] = block
        projects[phase, OWN * nz + iz] = block

    def project():
        both = jnp.dot(modes_t[...], halves(residual[...]), preferred_element_type=F32)
        return (both[:, :LANES] + both[:, LANES:])[:SUB]

    order_rows = jnp.broadcast_to(order_ref[...].astype(F32), (LANES, m))
    order_cols = order_rows.T
    lane = lax.broadcasted_iota(jnp.int32, (m, LANES), 1).astype(F32)
    for part in range(m // LANES):
        hit = order_cols == lane + float(part * LANES)
        perm[:, part * LANES:(part + 1) * LANES] = jnp.where(hit, 1.0, 0.0).astype(BF16)

    mode_pad[...] = jnp.zeros_like(mode_pad)
    mode_pad[pl.ds(0, nmode)] = modes_ref[...].astype(F32)
    repeated = jnp.concatenate([mode_pad[...]] * (LANES // SUB), axis=0).T.astype(BF16)
    rows = jnp.concatenate([load_ref[...], repeated], axis=1)
    both = jnp.dot(perm[...], rows, preferred_element_type=F32)
    image[...] = both[:, :LANES]
    own_modes[...] = both[:, LANES:]

    inverses[OWN] = jnp.zeros((csize, cwide), F32)
    inverses[OWN, :, pl.ds(0, csize)] = inverse_ref[...]
    publish(0, jnp.full((SUB, LANES), count_ref[0], jnp.int32).astype(F32))

    lines_x = 1 + jnp.where(ix > 0, 1, 0) + jnp.where(ix < nx - 1, 1, 0)
    lines_y = 1 + jnp.where(iy > 0, 1, 0) + jnp.where(iy < ny - 1, 1, 0)
    pl.semaphore_wait(barrier, lines_x * lines_y * nz - 1)

    every = range(len(SLOTS))
    send_slots(image, received, send_a, recv_a, every)
    send_blocks(0)
    for index, line in enumerate(LINES):
        if index != OWN:
            @pl.when(line_exists(line))
            def _(index=index):
                inverse_copy(index).start()
    send_slots(own_modes, far_modes, send_m, recv_m, every)

    for offset, begin, width in SLOTS:
        @pl.when(jnp.logical_not(slot_exists(offset)))
        def _(begin=begin, width=width):
            received[pl.ds(begin, width)] = jnp.zeros((width, LANES), F32)
            far_modes[pl.ds(begin, width)] = jnp.zeros((width, LANES), F32)
    for index, line in enumerate(LINES):
        @pl.when(jnp.logical_not(line_exists(line)))
        def _(index=index):
            projects[:, pl.ds(index * nz, nz)] = jnp.zeros((ITERS + 1, nz, SUB, LANES), F32)
            inverses[index] = jnp.zeros((csize, cwide), F32)

    modes_t[...] = own_modes[...].T[:modes_t.shape[0]].astype(BF16)
    tile = 2 * LANES
    order_row = order_ref[...]

    def transpose_tile(step, carry):
        base = pl.multiple_of(step * tile, tile)
        row = lax.broadcasted_iota(jnp.int32, (tile, m), 0) + base
        perm_t[pl.ds(base, tile)] = jnp.where(row == order_row, 1.0, 0.0).astype(BF16)
        return carry
    lax.fori_loop(0, m // tile, transpose_tile, 0)

    def first_product(step, carry):
        base = pl.multiple_of(step * tile, tile)
        half_packed[pl.ds(base, tile)] = jnp.dot(
            dual_ref[pl.ds(base, tile)], perm_t[...], preferred_element_type=F32).astype(BF16)
        return carry
    lax.fori_loop(0, m // tile, first_product, 0)

    wait_slots(image, received, send_a, recv_a)
    residual[...] = image[...] + received[...]
    wait_blocks(0)
    publish(1, project())
    send_blocks(1)

    def second_product(step, carry):
        base = pl.multiple_of(step * tile, tile)
        packed[pl.ds(base, tile)] = jnp.dot(
            perm[pl.ds(base, tile)], half_packed[...], preferred_element_type=F32).astype(BF16)
        return carry
    lax.fori_loop(0, m // tile, second_product, 0)

    select_pad[...] = jnp.zeros_like(select_pad)
    sub_index = lax.broadcasted_iota(jnp.int32, (SUB, cwide), 0).astype(F32)
    position = lax.broadcasted_iota(jnp.int32, (SUB, cwide), 1).astype(F32)
    for index in range(len(LINES)):
        start = jnp.zeros((SUB, cwide), F32)
        for t in range(nz):
            count = jnp.concatenate([projects[0, index * nz + t]] * (cwide // LANES), axis=1)
            hit = (position == start + sub_index) & (sub_index < count)
            chosen = jnp.where(hit, 1.0, 0.0)
            select_pad[index, pl.ds((t + 1) * SUB, SUB)] = chosen
            select_all[pl.ds((index * nz + t) * SUB, SUB)] = chosen
            start = start + count
    for index, line in enumerate(LINES):
        if index != OWN:
            @pl.when(line_exists(line))
            def _(index=index):
                inverse_copy(8 - index).wait_recv()
                inverse_copy(index).wait_send()
    total = coarse.shape[0] // 2
    lane_all = lax.broadcasted_iota(jnp.int32, (3 * SUB, len(LINES) * line_rows), 1)
    strips = []
    for index in range(len(LINES)):
        near = select_pad[index, pl.ds(pl.multiple_of(iz * SUB, SUB), 3 * SUB)]
        left = jnp.dot(near[:, :csize], inverses[index], precision=HIGHEST, preferred_element_type=F32)
        strip = lax.dot_general(left, select_all[...], (((1,), (1,)), ((), ())),
                                precision=HIGHEST, preferred_element_type=F32)
        inside = (lane_all >= index * line_rows) & (lane_all < (index + 1) * line_rows)
        strips.append(jnp.where(inside, strip, 0.0))
    strips.append(jnp.zeros((total - BLOCKS * SUB, len(LINES) * line_rows), F32))
    whole = jnp.concatenate(strips, axis=0)
    high = whole.astype(BF16)
    coarse[pl.ds(0, total)] = high
    coarse[pl.ds(total, total)] = (whole - high.astype(F32)).astype(BF16)

    wait_slots(own_modes, far_modes, send_m, recv_m)
    numbers = [(((o[0] + 1) * 3 + o[1] + 1) * 3 + o[2] + 1) for o, _, _ in SLOTS]
    row_block = jnp.concatenate(
        [jnp.full((SLOTS[k][2], LANES), numbers[k], jnp.int32) for k in every], axis=0)
    lane_row = lax.broadcasted_iota(jnp.int32, (m, LANES), 1)
    for part in range(total // LANES):
        block = (lane_row + part * LANES) // SUB
        value = jnp.where(block == row_block, far_modes[...],
                          jnp.where(block == BLOCKS // 2, own_modes[...], 0.0))
        wide[:, part * LANES:(part + 1) * LANES] = value.astype(BF16)

    direction[...] = jnp.zeros_like(direction)
    multipliers[...] = jnp.zeros_like(multipliers)
    faces = 6 * FACE
    pairs = coefficients()

    def iteration(step, carry):
        keep, gain = jnp.float32(pairs[0][0]), jnp.float32(pairs[0][1])
        for k in range(1, ITERS):
            keep = jnp.where(step == k, jnp.float32(pairs[k][0]), keep)
            gain = jnp.where(step == k, jnp.float32(pairs[k][1]), gain)
        wait_blocks(step + 1)
        line_projects = projects[step + 1].reshape(len(LINES) * line_rows, LANES)
        four = jnp.dot(coarse[...], halves(line_projects), preferred_element_type=F32)
        amplitude = four[:total, :LANES] + (four[:total, LANES:] + four[total:, :LANES])
        both = jnp.dot(wide[...], halves(amplitude), preferred_element_type=F32)
        corrected = residual[...] - (both[:, :LANES] + both[:, LANES:])
        now = keep * direction[...] + gain * corrected
        direction[...] = now
        multipliers[...] = multipliers[...] + now
        rounded = now.astype(BF16)
        image[pl.ds(0, faces)] = jnp.dot(packed[pl.ds(0, faces)], rounded, preferred_element_type=F32)
        send_slots(image, received, send_a, recv_a, range(6))
        image[pl.ds(faces, m - faces)] = jnp.dot(
            packed[pl.ds(faces, m - faces)], rounded, preferred_element_type=F32)
        send_slots(image, received, send_a, recv_a, range(6, len(SLOTS)))

        @pl.when(step == ITERS - 1)
        def _():
            pair = jnp.dot(perm_t[...], halves(multipliers[...]), preferred_element_type=F32)
            mult_out[...] = pair[:, :LANES] + pair[:, LANES:]

        wait_slots(image, received, send_a, recv_a)
        residual[...] = residual[...] - image[...] - received[...]

        @pl.when(step < ITERS - 1)
        def _():
            publish(step + 2, project())
            send_blocks(step + 2)
        return carry
    lax.fori_loop(0, ITERS, iteration, 0)

    pair = jnp.dot(perm_t[...], halves(residual[...]), preferred_element_type=F32)
    res_out[...] = pair[:, :LANES] + pair[:, LANES:]


def local(shape, dual_blocks, load_terms, row_order, mode_rows, mode_count, coarse_inverse):
    nz = shape[2]
    m, loads = load_terms.shape[3:]
    csize = coarse_inverse.shape[2]
    cwide = -(-csize // LANES) * LANES
    lines = len(LINES)
    line_rows = nz * SUB
    total = -(-BLOCKS * SUB // LANES) * LANES
    vmem = pl.BlockSpec(memory_space=pltpu.VMEM)
    smem = pl.BlockSpec(memory_space=pltpu.SMEM)
    rows = pltpu.VMEM((m, loads), F32)
    square = pltpu.VMEM((m, m), BF16)
    dma = pltpu.SemaphoreType.DMA
    slots = len(SLOTS)
    out = jax.ShapeDtypeStruct((m, loads), F32)
    multipliers, residual = pl.pallas_call(
        functools.partial(kernel, shape),
        out_shape=(out, out),
        in_specs=[vmem, vmem, vmem, vmem, smem, vmem],
        out_specs=(vmem, vmem),
        scratch_shapes=[
            square, square, square, square, rows, rows, rows, rows,
            pltpu.VMEM((m, total), BF16),
            rows, rows, rows,
            pltpu.VMEM((2 * SUB, m), BF16),
            pltpu.VMEM((SUB, m), F32),
            pltpu.VMEM((ITERS + 1, SUB, LANES), F32),
            pltpu.VMEM((ITERS + 1, lines * nz, SUB, LANES), F32),
            pltpu.VMEM((lines, csize, cwide), F32),
            pltpu.VMEM((lines, line_rows + 2 * SUB, cwide), F32),
            pltpu.VMEM((lines * line_rows, cwide), F32),
            pltpu.VMEM((2 * total, lines * line_rows), BF16),
            dma((slots,)), dma((slots,)), dma((slots,)), dma((slots,)),
            dma((lines,)), dma((ITERS + 1, lines)), dma((lines,)), dma((lines,)),
        ],
        compiler_params=pltpu.CompilerParams(
            collective_id=0, has_side_effects=True, vmem_limit_bytes=48 * 1024 * 1024),
    )(dual_blocks[0, 0, 0], load_terms[0, 0, 0], row_order[0, 0], mode_rows[0, 0, 0].T,
      mode_count.reshape(1), coarse_inverse[0, 0])
    return multipliers[None, None, None], residual[None, None, None]


def solution(mesh):
    shape = tuple(mesh.shape[name] for name in ("gx", "gy", "gz"))
    in_specs = (
        P("gx", "gy", "gz", None, None),
        P("gx", "gy", "gz", None, None),
        P("gx", "gy", "gz", None),
        P("gx", "gy", "gz", None, None),
        P("gx", "gy", "gz"),
        P("gx", "gy", None, None),
    )
    out_specs = (P("gx", "gy", "gz", None, None), P("gx", "gy", "gz", None, None))
    return jax.shard_map(functools.partial(local, shape), mesh=mesh, in_specs=in_specs,
                         out_specs=out_specs, check_vma=False)
```

```python
import functools

import jax
import jax.numpy as jnp
from jax import lax
from jax.experimental import pallas as pl
from jax.experimental.pallas import tpu as pltpu
from jax.sharding import PartitionSpec as P

FACE = 128
EDGE = 16
CORNER = 8
ITERS = 3
EIG_LOW = 0.5
EIG_HIGH = 6.0

MESH = pl.DeviceIdType.MESH
LANES = 128
VMEM_BYTES = 62 * 1024 * 1024
SUB = 8
F32 = jnp.float32
BF16 = jnp.bfloat16


def slot_table():
    slots = []
    begin = 0
    for weight, width in ((1, FACE), (2, EDGE), (3, CORNER)):
        for a in (-1, 0, 1):
            for b in (-1, 0, 1):
                for c in (-1, 0, 1):
                    if abs(a) + abs(b) + abs(c) == weight:
                        slots.append(((a, b, c), begin, width))
                        begin += width
    return slots


SLOTS = slot_table()
BEGIN = {offset: begin for offset, begin, _ in SLOTS}
LINES = [(a, b) for a in (-1, 0, 1) for b in (-1, 0, 1)]
OWN = 4
BLOCKS = 3 * len(LINES)


def coefficients():
    center = 0.5 * (EIG_HIGH + EIG_LOW)
    half = 0.5 * (EIG_HIGH - EIG_LOW)
    pairs = [(0.0, 1.0 / center)]
    rho = half / center
    for _ in range(1, ITERS):
        following = 1.0 / (2.0 * center / half - rho)
        pairs.append((following * rho, 2.0 * following / half))
        rho = following
    return pairs


def halves(x):
    high = x.astype(BF16)
    low = (x - high.astype(F32)).astype(BF16)
    return jnp.concatenate([high, low], axis=1)


def kernel(shape, dual_hbm, load_hbm, order_hbm, modes_hbm, count_ref, inverse_hbm,
           mult_hbm, res_hbm,
           mult_out, res_out, written, dual_ref, load_ref, order_ref, modes_ref, inverse_ref, fetched,
           perm, perm_t, half_packed, packed, image, received, own_modes, far_modes, wide,
           residual, direction, multipliers, modes_t, mode_pad,
           project_out, projects, inverses, select_pad, select_all, coarse,
           send_a, recv_a, send_m, recv_m, send_b, recv_b, send_i, recv_i):
    nx, ny, nz = shape
    ix, iy, iz = lax.axis_index("gx"), lax.axis_index("gy"), lax.axis_index("gz")
    m = dual_ref.shape[0]
    nmode = modes_ref.shape[0]
    csize = inverse_ref.shape[0]
    cwide = inverses.shape[2]
    line_rows = nz * SUB
    fetch = [pltpu.make_async_copy(source, target, fetched.at[k]) for k, (source, target) in enumerate(
        ((order_hbm, order_ref), (load_hbm, load_ref), (modes_hbm, modes_ref),
         (inverse_hbm, inverse_ref), (dual_hbm, dual_ref)))]
    for copy in fetch:
        copy.start()
    results = [pltpu.make_async_copy(mult_out, mult_hbm, written.at[0]),
               pltpu.make_async_copy(res_out, res_hbm, written.at[1])]
    barrier = pltpu.get_barrier_semaphore()

    def line_exists(line):
        a, b = line
        return (ix + a >= 0) & (ix + a < nx) & (iy + b >= 0) & (iy + b < ny)

    def slot_exists(offset):
        return line_exists(offset[:2]) & (iz + offset[2] >= 0) & (iz + offset[2] < nz)

    def each_device(line_index, action):
        def step(t, carry):
            if line_index == OWN:
                @pl.when(t != iz)
                def _():
                    action(t)
            else:
                action(t)
            return carry
        lax.fori_loop(0, nz, step, 0, unroll=nz <= 4)

    for index, line in enumerate(LINES):
        @pl.when(line_exists(line))
        def _(index=index, line=line):
            def greet(t):
                pl.semaphore_signal(barrier, inc=1, device_id=(ix + line[0], iy + line[1], t),
                                    device_id_type=MESH)
            each_device(index, greet)

    def slot_copy(source, target, send, recv, number):
        offset, begin, width = SLOTS[number]
        back = (-offset[0], -offset[1], -offset[2])
        return pltpu.make_async_remote_copy(
            src_ref=source.at[pl.ds(begin, width)],
            dst_ref=target.at[pl.ds(BEGIN[back], width)],
            send_sem=send.at[number],
            recv_sem=recv.at[[s[0] for s in SLOTS].index(back)],
            device_id=(ix + offset[0], iy + offset[1], iz + offset[2]),
            device_id_type=MESH)

    def slot_arrival(target, send, recv, number):
        offset, begin, width = SLOTS[number]
        return pltpu.make_async_remote_copy(
            src_ref=target.at[pl.ds(begin, width)],
            dst_ref=target.at[pl.ds(begin, width)],
            send_sem=send.at[number], recv_sem=recv.at[number],
            device_id=(ix + offset[0], iy + offset[1], iz + offset[2]),
            device_id_type=MESH)

    def send_slots(source, target, send, recv, numbers):
        for number in numbers:
            @pl.when(slot_exists(SLOTS[number][0]))
            def _(number=number):
                slot_copy(source, target, send, recv, number).start()

    def wait_slots(source, target, send, recv):
        for number in range(len(SLOTS)):
            @pl.when(slot_exists(SLOTS[number][0]))
            def _(number=number):
                slot_arrival(target, send, recv, number).wait_recv()
                slot_copy(source, target, send, recv, number).wait_send()

    def send_blocks(phase):
        for index, line in enumerate(LINES):
            @pl.when(line_exists(line))
            def _(index=index, line=line):
                def copy(t):
                    pltpu.make_async_remote_copy(
                        src_ref=project_out.at[phase],
                        dst_ref=projects.at[phase, (8 - index) * nz + iz],
                        send_sem=send_b.at[index],
                        recv_sem=recv_b.at[phase, 8 - index],
                        device_id=(ix + line[0], iy + line[1], t),
                        device_id_type=MESH).start()
                each_device(index, copy)

    def wait_blocks(phase):
        for index, line in enumerate(LINES):
            blocks = nz - 1 if index == OWN else nz
            if blocks == 0:
                continue
            @pl.when(line_exists(line))
            def _(index=index, line=line, blocks=blocks):
                span = projects.at[phase, pl.ds(index * nz, blocks)]
                arrival = pltpu.make_async_remote_copy(
                    src_ref=span, dst_ref=span,
                    send_sem=send_b.at[index], recv_sem=recv_b.at[phase, index],
                    device_id=(ix + line[0], iy + line[1], iz), device_id_type=MESH)
                arrival.wait_recv()
                arrival.wait_send()

    def inverse_copy(index):
        line = LINES[index]
        return pltpu.make_async_remote_copy(
            src_ref=inverses.at[OWN], dst_ref=inverses.at[8 - index],
            send_sem=send_i.at[index], recv_sem=recv_i.at[8 - index],
            device_id=(ix + line[0], iy + line[1], iz), device_id_type=MESH)

    def publish(phase, block):
        project_out[phase] = block
        projects[phase, OWN * nz + iz] = block

    def project():
        both = jnp.dot(modes_t[...], halves(residual[...]), preferred_element_type=F32)
        return (both[:, :LANES] + both[:, LANES:])[:SUB]

    fetch[0].wait()
    order_rows = jnp.broadcast_to(order_ref[...].astype(F32), (LANES, m))
    order_cols = order_rows.T
    lane = lax.broadcasted_iota(jnp.int32, (m, LANES), 1).astype(F32)
    for part in range(m // LANES):
        hit = order_cols == lane + float(part * LANES)
        perm[:, part * LANES:(part + 1) * LANES] = jnp.where(hit, 1.0, 0.0).astype(BF16)

    fetch[1].wait()
    fetch[2].wait()
    mode_pad[...] = jnp.zeros_like(mode_pad)
    mode_pad[pl.ds(0, nmode)] = modes_ref[...].astype(F32)
    repeated = jnp.concatenate([mode_pad[...]] * (LANES // SUB), axis=0).T.astype(BF16)
    rows = jnp.concatenate([load_ref[...], repeated], axis=1)
    both = jnp.dot(perm[...], rows, preferred_element_type=F32)
    image[...] = both[:, :LANES]
    own_modes[...] = both[:, LANES:]

    fetch[3].wait()
    inverses[OWN] = jnp.zeros((csize, cwide), F32)
    inverses[OWN, :, pl.ds(0, csize)] = inverse_ref[...]
    publish(0, jnp.full((SUB, LANES), count_ref[0], jnp.int32).astype(F32))

    lines_x = 1 + jnp.where(ix > 0, 1, 0) + jnp.where(ix < nx - 1, 1, 0)
    lines_y = 1 + jnp.where(iy > 0, 1, 0) + jnp.where(iy < ny - 1, 1, 0)
    pl.semaphore_wait(barrier, lines_x * lines_y * nz - 1)

    every = range(len(SLOTS))
    send_slots(image, received, send_a, recv_a, every)
    send_blocks(0)
    for index, line in enumerate(LINES):
        if index != OWN:
            @pl.when(line_exists(line))
            def _(index=index):
                inverse_copy(index).start()
    send_slots(own_modes, far_modes, send_m, recv_m, every)

    for offset, begin, width in SLOTS:
        @pl.when(jnp.logical_not(slot_exists(offset)))
        def _(begin=begin, width=width):
            received[pl.ds(begin, width)] = jnp.zeros((width, LANES), F32)
            far_modes[pl.ds(begin, width)] = jnp.zeros((width, LANES), F32)
    for index, line in enumerate(LINES):
        @pl.when(jnp.logical_not(line_exists(line)))
        def _(index=index):
            projects[:, pl.ds(index * nz, nz)] = jnp.zeros((ITERS + 1, nz, SUB, LANES), F32)
            inverses[index] = jnp.zeros((csize, cwide), F32)

    modes_t[...] = own_modes[...].T[:modes_t.shape[0]].astype(BF16)
    tile = 2 * LANES
    order_row = order_ref[...]

    def transpose_tile(step, carry):
        base = pl.multiple_of(step * tile, tile)
        row = lax.broadcasted_iota(jnp.int32, (tile, m), 0) + base
        perm_t[pl.ds(base, tile)] = jnp.where(row == order_row, 1.0, 0.0).astype(BF16)
        return carry
    lax.fori_loop(0, m // tile, transpose_tile, 0)

    fetch[4].wait()

    def first_product(step, carry):
        base = pl.multiple_of(step * tile, tile)
        half_packed[pl.ds(base, tile)] = jnp.dot(
            dual_ref[pl.ds(base, tile)], perm_t[...], preferred_element_type=F32).astype(BF16)
        return carry
    lax.fori_loop(0, m // tile, first_product, 0)

    wait_slots(image, received, send_a, recv_a)
    residual[...] = image[...] + received[...]
    wait_blocks(0)
    publish(1, project())
    send_blocks(1)

    def second_product(step, carry):
        base = pl.multiple_of(step * tile, tile)
        packed[pl.ds(base, tile)] = jnp.dot(
            perm[pl.ds(base, tile)], half_packed[...], preferred_element_type=F32).astype(BF16)
        return carry
    lax.fori_loop(0, m // tile, second_product, 0)

    select_pad[...] = jnp.zeros_like(select_pad)
    sub_index = lax.broadcasted_iota(jnp.int32, (SUB, cwide), 0).astype(F32)
    position = lax.broadcasted_iota(jnp.int32, (SUB, cwide), 1).astype(F32)
    for index in range(len(LINES)):
        start = jnp.zeros((SUB, cwide), F32)
        for t in range(nz):
            count = jnp.concatenate([projects[0, index * nz + t]] * (cwide // LANES), axis=1)
            hit = (position == start + sub_index) & (sub_index < count)
            chosen = jnp.where(hit, 1.0, 0.0)
            select_pad[index, pl.ds((t + 1) * SUB, SUB)] = chosen
            select_all[pl.ds((index * nz + t) * SUB, SUB)] = chosen
            start = start + count
    for index, line in enumerate(LINES):
        if index != OWN:
            @pl.when(line_exists(line))
            def _(index=index):
                inverse_copy(8 - index).wait_recv()
                inverse_copy(index).wait_send()
    total = coarse.shape[0] // 2
    lefts = []
    for index in range(len(LINES)):
        near = select_pad[index, pl.ds(pl.multiple_of(iz * SUB, SUB), 3 * SUB)]
        both = jnp.dot(near[:, :csize].astype(BF16), halves(inverses[index]), preferred_element_type=F32)
        lefts.append(both)
    lefts.append(jnp.zeros((total - BLOCKS * SUB, 2 * cwide), F32))
    lefts = jnp.concatenate(lefts, axis=0).astype(BF16)
    whole = jnp.zeros((total, len(LINES) * line_rows), F32)
    for part in range(2):
        whole = whole + lax.dot_general(
            lefts[:, part * cwide:(part + 1) * cwide], select_all[...].astype(BF16),
            (((1,), (1,)), ((), ())), preferred_element_type=F32)
    row_line = lax.broadcasted_iota(jnp.int32, whole.shape, 0) // (3 * SUB)
    lane_line = lax.broadcasted_iota(jnp.int32, whole.shape, 1) // line_rows
    whole = jnp.where(row_line == lane_line, whole, 0.0)
    high = whole.astype(BF16)
    coarse[pl.ds(0, total)] = high
    coarse[pl.ds(total, total)] = (whole - high.astype(F32)).astype(BF16)

    wait_slots(own_modes, far_modes, send_m, recv_m)
    numbers = [(((o[0] + 1) * 3 + o[1] + 1) * 3 + o[2] + 1) for o, _, _ in SLOTS]
    row_block = jnp.concatenate(
        [jnp.full((SLOTS[k][2], LANES), numbers[k], jnp.int32) for k in every], axis=0)
    lane_row = lax.broadcasted_iota(jnp.int32, (m, LANES), 1)
    for part in range(total // LANES):
        block = (lane_row + part * LANES) // SUB
        value = jnp.where(block == row_block, far_modes[...],
                          jnp.where(block == BLOCKS // 2, own_modes[...], 0.0))
        wide[:, part * LANES:(part + 1) * LANES] = value.astype(BF16)

    direction[...] = jnp.zeros_like(direction)
    multipliers[...] = jnp.zeros_like(multipliers)
    faces = 6 * FACE
    pairs = coefficients()

    def iteration(step, carry):
        keep, gain = jnp.float32(pairs[0][0]), jnp.float32(pairs[0][1])
        for k in range(1, ITERS):
            keep = jnp.where(step == k, jnp.float32(pairs[k][0]), keep)
            gain = jnp.where(step == k, jnp.float32(pairs[k][1]), gain)
        wait_blocks(step + 1)
        line_projects = projects[step + 1].reshape(len(LINES) * line_rows, LANES)
        four = jnp.dot(coarse[...], halves(line_projects), preferred_element_type=F32)
        amplitude = four[:total, :LANES] + (four[:total, LANES:] + four[total:, :LANES])
        both = jnp.dot(wide[...], halves(amplitude), preferred_element_type=F32)
        corrected = residual[...] - (both[:, :LANES] + both[:, LANES:])
        now = keep * direction[...] + gain * corrected
        direction[...] = now
        multipliers[...] = multipliers[...] + now
        rounded = now.astype(BF16)
        image[pl.ds(0, faces)] = jnp.dot(packed[pl.ds(0, faces)], rounded, preferred_element_type=F32)
        send_slots(image, received, send_a, recv_a, range(6))
        image[pl.ds(faces, m - faces)] = jnp.dot(
            packed[pl.ds(faces, m - faces)], rounded, preferred_element_type=F32)
        send_slots(image, received, send_a, recv_a, range(6, len(SLOTS)))

        @pl.when(step == ITERS - 1)
        def _():
            pair = jnp.dot(perm_t[...], halves(multipliers[...]), preferred_element_type=F32)
            mult_out[...] = pair[:, :LANES] + pair[:, LANES:]
            results[0].start()

        wait_slots(image, received, send_a, recv_a)
        residual[...] = residual[...] - image[...] - received[...]

        @pl.when(step < ITERS - 1)
        def _():
            publish(step + 2, project())
            send_blocks(step + 2)
        return carry
    lax.fori_loop(0, ITERS, iteration, 0)

    pair = jnp.dot(perm_t[...], halves(residual[...]), preferred_element_type=F32)
    res_out[...] = pair[:, :LANES] + pair[:, LANES:]
    results[1].start()
    results[0].wait()
    results[1].wait()


def write_out(mult_ref, res_ref, mult_hbm, res_hbm, written):
    copies = [pltpu.make_async_copy(mult_ref, mult_hbm, written.at[0]),
              pltpu.make_async_copy(res_ref, res_hbm, written.at[1])]
    for copy in copies:
        copy.start()
    for copy in copies:
        copy.wait()


def local(shape, dual_blocks, load_terms, row_order, mode_rows, mode_count, coarse_inverse):
    nz = shape[2]
    m, loads = load_terms.shape[3:]
    csize = coarse_inverse.shape[2]
    cwide = -(-csize // LANES) * LANES
    lines = len(LINES)
    line_rows = nz * SUB
    total = -(-BLOCKS * SUB // LANES) * LANES
    hbm = pl.BlockSpec(memory_space=pltpu.HBM)
    smem = pl.BlockSpec(memory_space=pltpu.SMEM)
    rows = pltpu.VMEM((m, loads), F32)
    square = pltpu.VMEM((m, m), BF16)
    dma = pltpu.SemaphoreType.DMA
    slots = len(SLOTS)
    out = jax.ShapeDtypeStruct((m, loads), F32)
    multipliers, residual = pl.pallas_call(
        functools.partial(kernel, shape),
        out_shape=(out, out),
        in_specs=[hbm, hbm, hbm, hbm, smem, hbm],
        out_specs=(hbm, hbm),
        scratch_shapes=[
            rows, rows, dma((2,)), square, pltpu.VMEM((m, loads), BF16), pltpu.VMEM((1, m), jnp.int32),
            pltpu.VMEM((mode_rows.shape[4], m), BF16), pltpu.VMEM((csize, csize), F32), dma((5,)),
            square, square, square, square, rows, rows, rows, rows,
            pltpu.VMEM((m, total), BF16),
            rows, rows, rows,
            pltpu.VMEM((2 * SUB, m), BF16),
            pltpu.VMEM((SUB, m), F32),
            pltpu.VMEM((ITERS + 1, SUB, LANES), F32),
            pltpu.VMEM((ITERS + 1, lines * nz, SUB, LANES), F32),
            pltpu.VMEM((lines, csize, cwide), F32),
            pltpu.VMEM((lines, line_rows + 2 * SUB, cwide), F32),
            pltpu.VMEM((lines * line_rows, cwide), F32),
            pltpu.VMEM((2 * total, lines * line_rows), BF16),
            dma((slots,)), dma((slots,)), dma((slots,)), dma((slots,)),
            dma((lines,)), dma((ITERS + 1, lines)), dma((lines,)), dma((lines,)),
        ],
        compiler_params=pltpu.CompilerParams(
            collective_id=0, has_side_effects=True, vmem_limit_bytes=VMEM_BYTES),
    )(dual_blocks[0, 0, 0], load_terms[0, 0, 0], row_order[0, 0], mode_rows[0, 0, 0].T,
      mode_count.reshape(1), coarse_inverse[0, 0])
    multipliers, residual = pl.pallas_call(
        write_out,
        out_shape=(out, out),
        in_specs=[hbm, hbm],
        out_specs=(hbm, hbm),
        scratch_shapes=[dma((2,))],
        compiler_params=pltpu.CompilerParams(vmem_limit_bytes=VMEM_BYTES),
    )(multipliers, residual)
    return multipliers[None, None, None], residual[None, None, None]


def solution(mesh):
    shape = tuple(mesh.shape[name] for name in ("gx", "gy", "gz"))
    in_specs = (
        P("gx", "gy", "gz", None, None),
        P("gx", "gy", "gz", None, None),
        P("gx", "gy", "gz", None),
        P("gx", "gy", "gz", None, None),
        P("gx", "gy", "gz"),
        P("gx", "gy", None, None),
    )
    out_specs = (P("gx", "gy", "gz", None, None), P("gx", "gy", "gz", None, None))
    return jax.shard_map(functools.partial(local, shape), mesh=mesh, in_specs=in_specs,
                         out_specs=out_specs, check_vma=False)
```

```python
import functools

import jax
import jax.numpy as jnp
from jax import lax
from jax.experimental import pallas as pl
from jax.experimental.pallas import tpu as pltpu
from jax.sharding import PartitionSpec as P

FACE = 128
EDGE = 16
CORNER = 8
ITERS = 3
EIG_LOW = 0.5
EIG_HIGH = 6.0

MESH = pl.DeviceIdType.MESH
LANES = 128
VMEM_BYTES = 62 * 1024 * 1024
SUB = 8
F32 = jnp.float32
BF16 = jnp.bfloat16


def slot_table():
    slots = []
    begin = 0
    for weight, width in ((1, FACE), (2, EDGE), (3, CORNER)):
        for a in (-1, 0, 1):
            for b in (-1, 0, 1):
                for c in (-1, 0, 1):
                    if abs(a) + abs(b) + abs(c) == weight:
                        slots.append(((a, b, c), begin, width))
                        begin += width
    return slots


SLOTS = slot_table()
BEGIN = {offset: begin for offset, begin, _ in SLOTS}
LINES = [(a, b) for a in (-1, 0, 1) for b in (-1, 0, 1)]
OWN = 4
BLOCKS = 3 * len(LINES)


def coefficients():
    center = 0.5 * (EIG_HIGH + EIG_LOW)
    half = 0.5 * (EIG_HIGH - EIG_LOW)
    pairs = [(0.0, 1.0 / center)]
    rho = half / center
    for _ in range(1, ITERS):
        following = 1.0 / (2.0 * center / half - rho)
        pairs.append((following * rho, 2.0 * following / half))
        rho = following
    return pairs


def halves(x):
    high = x.astype(BF16)
    low = (x - high.astype(F32)).astype(BF16)
    return jnp.concatenate([high, low], axis=1)


def kernel(shape, dual_hbm, load_hbm, order_hbm, modes_hbm, count_ref, inverse_hbm,
           mult_hbm, res_hbm,
           mult_out, res_out, written, dual_ref, load_ref, order_ref, modes_ref, inverse_ref, fetched,
           perm, perm_t, half_packed, packed, image, received, own_modes, far_modes, wide,
           residual, direction, multipliers, modes_t, mode_pad,
           project_out, projects, inverses, select_pad, select_all, coarse,
           send_a, recv_a, send_m, recv_m, send_b, recv_b, send_i, recv_i):
    nx, ny, nz = shape
    ix, iy, iz = lax.axis_index("gx"), lax.axis_index("gy"), lax.axis_index("gz")
    m = dual_ref.shape[0]
    nmode = modes_ref.shape[0]
    csize = inverse_ref.shape[0]
    cwide = inverses.shape[2]
    line_rows = nz * SUB
    fetch = [pltpu.make_async_copy(source, target, fetched.at[k]) for k, (source, target) in enumerate(
        ((order_hbm, order_ref), (load_hbm, load_ref), (modes_hbm, modes_ref),
         (inverse_hbm, inverse_ref), (dual_hbm, dual_ref)))]
    for copy in fetch:
        copy.start()
    results = [pltpu.make_async_copy(mult_out, mult_hbm, written.at[0]),
               pltpu.make_async_copy(res_out, res_hbm, written.at[1])]
    barrier = pltpu.get_barrier_semaphore()

    def line_exists(line):
        a, b = line
        return (ix + a >= 0) & (ix + a < nx) & (iy + b >= 0) & (iy + b < ny)

    def slot_exists(offset):
        return line_exists(offset[:2]) & (iz + offset[2] >= 0) & (iz + offset[2] < nz)

    def each_device(line_index, action):
        def step(t, carry):
            if line_index == OWN:
                @pl.when(t != iz)
                def _():
                    action(t)
            else:
                action(t)
            return carry
        lax.fori_loop(0, nz, step, 0, unroll=nz <= 4)

    for index, line in enumerate(LINES):
        @pl.when(line_exists(line))
        def _(index=index, line=line):
            def greet(t):
                pl.semaphore_signal(barrier, inc=1, device_id=(ix + line[0], iy + line[1], t),
                                    device_id_type=MESH)
            each_device(index, greet)

    def slot_copy(source, target, send, recv, number):
        offset, begin, width = SLOTS[number]
        back = (-offset[0], -offset[1], -offset[2])
        return pltpu.make_async_remote_copy(
            src_ref=source.at[pl.ds(begin, width)],
            dst_ref=target.at[pl.ds(BEGIN[back], width)],
            send_sem=send.at[number],
            recv_sem=recv.at[[s[0] for s in SLOTS].index(back)],
            device_id=(ix + offset[0], iy + offset[1], iz + offset[2]),
            device_id_type=MESH)

    def slot_arrival(target, send, recv, number):
        offset, begin, width = SLOTS[number]
        return pltpu.make_async_remote_copy(
            src_ref=target.at[pl.ds(begin, width)],
            dst_ref=target.at[pl.ds(begin, width)],
            send_sem=send.at[number], recv_sem=recv.at[number],
            device_id=(ix + offset[0], iy + offset[1], iz + offset[2]),
            device_id_type=MESH)

    def send_slots(source, target, send, recv, numbers):
        for number in numbers:
            @pl.when(slot_exists(SLOTS[number][0]))
            def _(number=number):
                slot_copy(source, target, send, recv, number).start()

    def wait_slots(source, target, send, recv):
        for number in range(len(SLOTS)):
            @pl.when(slot_exists(SLOTS[number][0]))
            def _(number=number):
                slot_arrival(target, send, recv, number).wait_recv()
                slot_copy(source, target, send, recv, number).wait_send()

    def send_blocks(phase):
        for index, line in enumerate(LINES):
            @pl.when(line_exists(line))
            def _(index=index, line=line):
                def copy(t):
                    pltpu.make_async_remote_copy(
                        src_ref=project_out.at[phase],
                        dst_ref=projects.at[phase, (8 - index) * nz + iz],
                        send_sem=send_b.at[index],
                        recv_sem=recv_b.at[phase, 8 - index],
                        device_id=(ix + line[0], iy + line[1], t),
                        device_id_type=MESH).start()
                each_device(index, copy)

    def wait_blocks(phase):
        for index, line in enumerate(LINES):
            blocks = nz - 1 if index == OWN else nz
            if blocks == 0:
                continue
            @pl.when(line_exists(line))
            def _(index=index, line=line, blocks=blocks):
                span = projects.at[phase, pl.ds(index * nz, blocks)]
                arrival = pltpu.make_async_remote_copy(
                    src_ref=span, dst_ref=span,
                    send_sem=send_b.at[index], recv_sem=recv_b.at[phase, index],
                    device_id=(ix + line[0], iy + line[1], iz), device_id_type=MESH)
                arrival.wait_recv()
                arrival.wait_send()

    def inverse_copy(index):
        line = LINES[index]
        return pltpu.make_async_remote_copy(
            src_ref=inverses.at[OWN], dst_ref=inverses.at[8 - index],
            send_sem=send_i.at[index], recv_sem=recv_i.at[8 - index],
            device_id=(ix + line[0], iy + line[1], iz), device_id_type=MESH)

    def publish(phase, block):
        project_out[phase] = block
        projects[phase, OWN * nz + iz] = block

    def project():
        both = jnp.dot(modes_t[...], halves(residual[...]), preferred_element_type=F32)
        return (both[:, :LANES] + both[:, LANES:])[:SUB]

    fetch[0].wait()
    order_rows = jnp.broadcast_to(order_ref[...].astype(F32), (LANES, m))
    order_cols = order_rows.T
    lane = lax.broadcasted_iota(jnp.int32, (m, LANES), 1).astype(F32)
    for part in range(m // LANES):
        hit = order_cols == lane + float(part * LANES)
        perm[:, part * LANES:(part + 1) * LANES] = jnp.where(hit, 1.0, 0.0).astype(BF16)

    fetch[1].wait()
    fetch[2].wait()
    mode_pad[...] = jnp.zeros_like(mode_pad)
    mode_pad[pl.ds(0, nmode)] = modes_ref[...].astype(F32)
    repeated = jnp.concatenate([mode_pad[...]] * (LANES // SUB), axis=0).T.astype(BF16)
    rows = jnp.concatenate([load_ref[...], repeated], axis=1)
    both = jnp.dot(perm[...], rows, preferred_element_type=F32)
    image[...] = both[:, :LANES]
    own_modes[...] = both[:, LANES:]

    fetch[3].wait()
    inverses[OWN] = jnp.zeros((csize, cwide), F32)
    inverses[OWN, :, pl.ds(0, csize)] = inverse_ref[...]
    publish(0, jnp.full((SUB, LANES), count_ref[0], jnp.int32).astype(F32))

    lines_x = 1 + jnp.where(ix > 0, 1, 0) + jnp.where(ix < nx - 1, 1, 0)
    lines_y = 1 + jnp.where(iy > 0, 1, 0) + jnp.where(iy < ny - 1, 1, 0)
    pl.semaphore_wait(barrier, lines_x * lines_y * nz - 1)

    every = range(len(SLOTS))
    send_slots(image, received, send_a, recv_a, every)
    send_blocks(0)
    for index, line in enumerate(LINES):
        if index != OWN:
            @pl.when(line_exists(line))
            def _(index=index):
                inverse_copy(index).start()
    send_slots(own_modes, far_modes, send_m, recv_m, every)

    for offset, begin, width in SLOTS:
        @pl.when(jnp.logical_not(slot_exists(offset)))
        def _(begin=begin, width=width):
            received[pl.ds(begin, width)] = jnp.zeros((width, LANES), F32)
            far_modes[pl.ds(begin, width)] = jnp.zeros((width, LANES), F32)
    for index, line in enumerate(LINES):
        @pl.when(jnp.logical_not(line_exists(line)))
        def _(index=index):
            projects[:, pl.ds(index * nz, nz)] = jnp.zeros((ITERS + 1, nz, SUB, LANES), F32)
            inverses[index] = jnp.zeros((csize, cwide), F32)

    modes_t[...] = own_modes[...].T[:modes_t.shape[0]].astype(BF16)
    tile = 2 * LANES
    order_row = order_ref[...]

    def transpose_tile(step, carry):
        base = pl.multiple_of(step * tile, tile)
        row = lax.broadcasted_iota(jnp.int32, (tile, m), 0) + base
        perm_t[pl.ds(base, tile)] = jnp.where(row == order_row, 1.0, 0.0).astype(BF16)
        return carry
    lax.fori_loop(0, m // tile, transpose_tile, 0)

    fetch[4].wait()

    def first_product(step, carry):
        base = pl.multiple_of(step * tile, tile)
        half_packed[pl.ds(base, tile)] = jnp.dot(
            dual_ref[pl.ds(base, tile)], perm_t[...], preferred_element_type=F32).astype(BF16)
        return carry
    lax.fori_loop(0, m // tile, first_product, 0)

    wait_slots(image, received, send_a, recv_a)
    residual[...] = image[...] + received[...]
    wait_blocks(0)
    publish(1, project())
    send_blocks(1)

    def second_product(step, carry):
        base = pl.multiple_of(step * tile, tile)
        packed[pl.ds(base, tile)] = jnp.dot(
            perm[pl.ds(base, tile)], half_packed[...], preferred_element_type=F32).astype(BF16)
        return carry
    lax.fori_loop(0, m // tile, second_product, 0)

    select_pad[...] = jnp.zeros_like(select_pad)
    sub_index = lax.broadcasted_iota(jnp.int32, (SUB, cwide), 0).astype(F32)
    position = lax.broadcasted_iota(jnp.int32, (SUB, cwide), 1).astype(F32)
    for index in range(len(LINES)):
        start = jnp.zeros((SUB, cwide), F32)
        for t in range(nz):
            count = jnp.concatenate([projects[0, index * nz + t]] * (cwide // LANES), axis=1)
            hit = (position == start + sub_index) & (sub_index < count)
            chosen = jnp.where(hit, 1.0, 0.0)
            select_pad[index, pl.ds((t + 1) * SUB, SUB)] = chosen
            select_all[pl.ds((index * nz + t) * SUB, SUB)] = chosen
            start = start + count
    for index, line in enumerate(LINES):
        if index != OWN:
            @pl.when(line_exists(line))
            def _(index=index):
                inverse_copy(8 - index).wait_recv()
                inverse_copy(index).wait_send()
    total = coarse.shape[0] // 2
    lefts = []
    for index in range(len(LINES)):
        near = select_pad[index, pl.ds(pl.multiple_of(iz * SUB, SUB), 3 * SUB)]
        both = jnp.dot(near[:, :csize].astype(BF16), halves(inverses[index]), preferred_element_type=F32)
        lefts.append(both)
    lefts.append(jnp.zeros((total - BLOCKS * SUB, 2 * cwide), F32))
    lefts = jnp.concatenate(lefts, axis=0).astype(BF16)
    whole = jnp.zeros((total, len(LINES) * line_rows), F32)
    for part in range(2):
        whole = whole + lax.dot_general(
            lefts[:, part * cwide:(part + 1) * cwide], select_all[...].astype(BF16),
            (((1,), (1,)), ((), ())), preferred_element_type=F32)
    row_line = lax.broadcasted_iota(jnp.int32, whole.shape, 0) // (3 * SUB)
    lane_line = lax.broadcasted_iota(jnp.int32, whole.shape, 1) // line_rows
    whole = jnp.where(row_line == lane_line, whole, 0.0)
    high = whole.astype(BF16)
    coarse[pl.ds(0, total)] = high
    coarse[pl.ds(total, total)] = (whole - high.astype(F32)).astype(BF16)

    wait_slots(own_modes, far_modes, send_m, recv_m)
    numbers = [(((o[0] + 1) * 3 + o[1] + 1) * 3 + o[2] + 1) for o, _, _ in SLOTS]
    row_block = jnp.concatenate(
        [jnp.full((SLOTS[k][2], LANES), numbers[k], jnp.int32) for k in every], axis=0)
    lane_row = lax.broadcasted_iota(jnp.int32, (m, LANES), 1)
    for part in range(total // LANES):
        block = (lane_row + part * LANES) // SUB
        value = jnp.where(block == row_block, far_modes[...],
                          jnp.where(block == BLOCKS // 2, own_modes[...], 0.0))
        wide[:, part * LANES:(part + 1) * LANES] = value.astype(BF16)

    direction[...] = jnp.zeros_like(direction)
    multipliers[...] = jnp.zeros_like(multipliers)
    faces = 6 * FACE
    pairs = coefficients()

    def iteration(step, carry):
        keep, gain = jnp.float32(pairs[0][0]), jnp.float32(pairs[0][1])
        for k in range(1, ITERS):
            keep = jnp.where(step == k, jnp.float32(pairs[k][0]), keep)
            gain = jnp.where(step == k, jnp.float32(pairs[k][1]), gain)
        wait_blocks(step + 1)
        line_projects = projects[step + 1].reshape(len(LINES) * line_rows, LANES)
        four = jnp.dot(coarse[...], halves(line_projects), preferred_element_type=F32)
        amplitude = four[:total, :LANES] + (four[:total, LANES:] + four[total:, :LANES])
        both = jnp.dot(wide[...], halves(amplitude), preferred_element_type=F32)
        corrected = residual[...] - (both[:, :LANES] + both[:, LANES:])
        now = keep * direction[...] + gain * corrected
        direction[...] = now
        multipliers[...] = multipliers[...] + now
        rounded = now.astype(BF16)
        image[pl.ds(0, faces)] = jnp.dot(packed[pl.ds(0, faces)], rounded, preferred_element_type=F32)
        send_slots(image, received, send_a, recv_a, range(6))
        image[pl.ds(faces, m - faces)] = jnp.dot(
            packed[pl.ds(faces, m - faces)], rounded, preferred_element_type=F32)
        send_slots(image, received, send_a, recv_a, range(6, len(SLOTS)))

        @pl.when(step == ITERS - 1)
        def _():
            pair = jnp.dot(perm_t[...], halves(multipliers[...]), preferred_element_type=F32)
            mult_out[...] = pair[:, :LANES] + pair[:, LANES:]
            results[0].start()

        wait_slots(image, received, send_a, recv_a)
        residual[...] = residual[...] - image[...] - received[...]

        @pl.when(step < ITERS - 1)
        def _():
            publish(step + 2, project())
            send_blocks(step + 2)
        return carry
    lax.fori_loop(0, ITERS, iteration, 0)

    pair = jnp.dot(perm_t[...], halves(residual[...]), preferred_element_type=F32)
    res_out[...] = pair[:, :LANES] + pair[:, LANES:]
    results[1].start()
    results[0].wait()
    results[1].wait()


def write_out(mult_ref, res_ref, mult_hbm, res_hbm, mult_held, res_held, read, written):
    inward = [pltpu.make_async_copy(mult_ref, mult_held, read.at[0]),
              pltpu.make_async_copy(res_ref, res_held, read.at[1])]
    outward = [pltpu.make_async_copy(mult_held, mult_hbm, written.at[0]),
               pltpu.make_async_copy(res_held, res_hbm, written.at[1])]
    for copy in inward:
        copy.start()
    for first, second in zip(inward, outward):
        first.wait()
        second.start()
    for copy in outward:
        copy.wait()


def local(shape, dual_blocks, load_terms, row_order, mode_rows, mode_count, coarse_inverse):
    nz = shape[2]
    m, loads = load_terms.shape[3:]
    csize = coarse_inverse.shape[2]
    cwide = -(-csize // LANES) * LANES
    lines = len(LINES)
    line_rows = nz * SUB
    total = -(-BLOCKS * SUB // LANES) * LANES
    hbm = pl.BlockSpec(memory_space=pltpu.HBM)
    smem = pl.BlockSpec(memory_space=pltpu.SMEM)
    rows = pltpu.VMEM((m, loads), F32)
    square = pltpu.VMEM((m, m), BF16)
    dma = pltpu.SemaphoreType.DMA
    slots = len(SLOTS)
    out = jax.ShapeDtypeStruct((m, loads), F32)
    multipliers, residual = pl.pallas_call(
        functools.partial(kernel, shape),
        out_shape=(out, out),
        in_specs=[hbm, hbm, hbm, hbm, smem, hbm],
        out_specs=(hbm, hbm),
        scratch_shapes=[
            rows, rows, dma((2,)), square, pltpu.VMEM((m, loads), BF16), pltpu.VMEM((1, m), jnp.int32),
            pltpu.VMEM((mode_rows.shape[4], m), BF16), pltpu.VMEM((csize, csize), F32), dma((5,)),
            square, square, square, square, rows, rows, rows, rows,
            pltpu.VMEM((m, total), BF16),
            rows, rows, rows,
            pltpu.VMEM((2 * SUB, m), BF16),
            pltpu.VMEM((SUB, m), F32),
            pltpu.VMEM((ITERS + 1, SUB, LANES), F32),
            pltpu.VMEM((ITERS + 1, lines * nz, SUB, LANES), F32),
            pltpu.VMEM((lines, csize, cwide), F32),
            pltpu.VMEM((lines, line_rows + 2 * SUB, cwide), F32),
            pltpu.VMEM((lines * line_rows, cwide), F32),
            pltpu.VMEM((2 * total, lines * line_rows), BF16),
            dma((slots,)), dma((slots,)), dma((slots,)), dma((slots,)),
            dma((lines,)), dma((ITERS + 1, lines)), dma((lines,)), dma((lines,)),
        ],
        compiler_params=pltpu.CompilerParams(
            collective_id=0, has_side_effects=True, vmem_limit_bytes=VMEM_BYTES),
    )(dual_blocks[0, 0, 0], load_terms[0, 0, 0], row_order[0, 0], mode_rows[0, 0, 0].T,
      mode_count.reshape(1), coarse_inverse[0, 0])
    multipliers, residual = pl.pallas_call(
        write_out,
        out_shape=(out, out),
        in_specs=[hbm, hbm],
        out_specs=(hbm, hbm),
        scratch_shapes=[rows, rows, dma((2,)), dma((2,))],
        compiler_params=pltpu.CompilerParams(vmem_limit_bytes=VMEM_BYTES),
    )(multipliers, residual)
    return multipliers[None, None, None], residual[None, None, None]


def solution(mesh):
    shape = tuple(mesh.shape[name] for name in ("gx", "gy", "gz"))
    in_specs = (
        P("gx", "gy", "gz", None, None),
        P("gx", "gy", "gz", None, None),
        P("gx", "gy", "gz", None),
        P("gx", "gy", "gz", None, None),
        P("gx", "gy", "gz"),
        P("gx", "gy", None, None),
    )
    out_specs = (P("gx", "gy", "gz", None, None), P("gx", "gy", "gz", None, None))
    return jax.shard_map(functools.partial(local, shape), mesh=mesh, in_specs=in_specs,
                         out_specs=out_specs, check_vma=False)
```

```python
import functools

import jax
import jax.numpy as jnp
from jax import lax
from jax.experimental import pallas as pl
from jax.experimental.pallas import tpu as pltpu
from jax.sharding import PartitionSpec as P

FACE = 128
EDGE = 16
CORNER = 8
ITERS = 3
EIG_LOW = 0.5
EIG_HIGH = 6.0

MESH = pl.DeviceIdType.MESH
LANES = 128
VMEM_BYTES = 62 * 1024 * 1024
SUB = 8
F32 = jnp.float32
BF16 = jnp.bfloat16


def slot_table():
    slots = []
    begin = 0
    for weight, width in ((1, FACE), (2, EDGE), (3, CORNER)):
        for a in (-1, 0, 1):
            for b in (-1, 0, 1):
                for c in (-1, 0, 1):
                    if abs(a) + abs(b) + abs(c) == weight:
                        slots.append(((a, b, c), begin, width))
                        begin += width
    return slots


SLOTS = slot_table()
BEGIN = {offset: begin for offset, begin, _ in SLOTS}
LINES = [(a, b) for a in (-1, 0, 1) for b in (-1, 0, 1)]
OWN = 4
BLOCKS = 3 * len(LINES)


def coefficients():
    center = 0.5 * (EIG_HIGH + EIG_LOW)
    half = 0.5 * (EIG_HIGH - EIG_LOW)
    pairs = [(0.0, 1.0 / center)]
    rho = half / center
    for _ in range(1, ITERS):
        following = 1.0 / (2.0 * center / half - rho)
        pairs.append((following * rho, 2.0 * following / half))
        rho = following
    return pairs


def halves(x):
    high = x.astype(BF16)
    low = (x - high.astype(F32)).astype(BF16)
    return jnp.concatenate([high, low], axis=1)


def kernel(shape, dual_hbm, load_hbm, order_hbm, modes_hbm, count_ref, inverse_hbm,
           mult_hbm, res_hbm,
           mult_out, res_out, written, dual_ref, load_ref, order_ref, modes_ref, inverse_ref, fetched,
           perm, perm_t, half_packed, packed, image, received, own_modes, far_modes, wide,
           wide_t, shares, arrived, line_project,
           residual, direction, multipliers, modes_t, mode_pad,
           project_out, projects, inverses, select_pad, select_all, coarse,
           send_a, recv_a, send_m, recv_m, send_c, recv_c, send_b, recv_b, send_i, recv_i):
    nx, ny, nz = shape
    ix, iy, iz = lax.axis_index("gx"), lax.axis_index("gy"), lax.axis_index("gz")
    numbers = [(((o[0] + 1) * 3 + o[1] + 1) * 3 + o[2] + 1) for o, _, _ in SLOTS]
    m = dual_ref.shape[0]
    nmode = modes_ref.shape[0]
    csize = inverse_ref.shape[0]
    cwide = inverses.shape[2]
    line_rows = nz * SUB
    fetch = [pltpu.make_async_copy(source, target, fetched.at[k]) for k, (source, target) in enumerate(
        ((order_hbm, order_ref), (load_hbm, load_ref), (modes_hbm, modes_ref),
         (inverse_hbm, inverse_ref), (dual_hbm, dual_ref)))]
    for copy in fetch:
        copy.start()
    results = [pltpu.make_async_copy(mult_out, mult_hbm, written.at[0]),
               pltpu.make_async_copy(res_out, res_hbm, written.at[1])]
    barrier = pltpu.get_barrier_semaphore()

    def line_exists(line):
        a, b = line
        return (ix + a >= 0) & (ix + a < nx) & (iy + b >= 0) & (iy + b < ny)

    def slot_exists(offset):
        return line_exists(offset[:2]) & (iz + offset[2] >= 0) & (iz + offset[2] < nz)

    def each_device(line_index, action):
        def step(t, carry):
            if line_index == OWN:
                @pl.when(t != iz)
                def _():
                    action(t)
            else:
                action(t)
            return carry
        lax.fori_loop(0, nz, step, 0, unroll=nz <= 4)

    for index, line in enumerate(LINES):
        @pl.when(line_exists(line))
        def _(index=index, line=line):
            def greet(t):
                pl.semaphore_signal(barrier, inc=1, device_id=(ix + line[0], iy + line[1], t),
                                    device_id_type=MESH)
            each_device(index, greet)

    def slot_copy(source, target, send, recv, number):
        offset, begin, width = SLOTS[number]
        back = (-offset[0], -offset[1], -offset[2])
        return pltpu.make_async_remote_copy(
            src_ref=source.at[pl.ds(begin, width)],
            dst_ref=target.at[pl.ds(BEGIN[back], width)],
            send_sem=send.at[number],
            recv_sem=recv.at[[s[0] for s in SLOTS].index(back)],
            device_id=(ix + offset[0], iy + offset[1], iz + offset[2]),
            device_id_type=MESH)

    def slot_arrival(target, send, recv, number):
        offset, begin, width = SLOTS[number]
        return pltpu.make_async_remote_copy(
            src_ref=target.at[pl.ds(begin, width)],
            dst_ref=target.at[pl.ds(begin, width)],
            send_sem=send.at[number], recv_sem=recv.at[number],
            device_id=(ix + offset[0], iy + offset[1], iz + offset[2]),
            device_id_type=MESH)

    def send_slots(source, target, send, recv, numbers):
        for number in numbers:
            @pl.when(slot_exists(SLOTS[number][0]))
            def _(number=number):
                slot_copy(source, target, send, recv, number).start()

    def wait_slots(source, target, send, recv):
        for number in range(len(SLOTS)):
            @pl.when(slot_exists(SLOTS[number][0]))
            def _(number=number):
                slot_arrival(target, send, recv, number).wait_recv()
                slot_copy(source, target, send, recv, number).wait_send()

    def send_blocks(phase):
        for index, line in enumerate(LINES):
            @pl.when(line_exists(line))
            def _(index=index, line=line):
                def copy(t):
                    pltpu.make_async_remote_copy(
                        src_ref=project_out.at[phase],
                        dst_ref=projects.at[phase, (8 - index) * nz + iz],
                        send_sem=send_b.at[index],
                        recv_sem=recv_b.at[phase, 8 - index],
                        device_id=(ix + line[0], iy + line[1], t),
                        device_id_type=MESH).start()
                each_device(index, copy)

    def wait_blocks(phase):
        for index, line in enumerate(LINES):
            blocks = nz - 1 if index == OWN else nz
            if blocks == 0:
                continue
            @pl.when(line_exists(line))
            def _(index=index, line=line, blocks=blocks):
                span = projects.at[phase, pl.ds(index * nz, blocks)]
                arrival = pltpu.make_async_remote_copy(
                    src_ref=span, dst_ref=span,
                    send_sem=send_b.at[index], recv_sem=recv_b.at[phase, index],
                    device_id=(ix + line[0], iy + line[1], iz), device_id_type=MESH)
                arrival.wait_recv()
                arrival.wait_send()

    def inverse_copy(index):
        line = LINES[index]
        return pltpu.make_async_remote_copy(
            src_ref=inverses.at[OWN], dst_ref=inverses.at[8 - index],
            send_sem=send_i.at[index], recv_sem=recv_i.at[8 - index],
            device_id=(ix + line[0], iy + line[1], iz), device_id_type=MESH)

    def share_copy(number):
        offset = SLOTS[number][0]
        other = [s[0] for s in SLOTS].index((-offset[0], -offset[1], -offset[2]))
        return pltpu.make_async_remote_copy(
            src_ref=shares.at[numbers[number]], dst_ref=arrived.at[other],
            send_sem=send_c.at[number], recv_sem=recv_c.at[other],
            device_id=(ix + offset[0], iy + offset[1], iz + offset[2]), device_id_type=MESH)

    def share_arrival(number):
        offset = SLOTS[number][0]
        return pltpu.make_async_remote_copy(
            src_ref=arrived.at[number], dst_ref=arrived.at[number],
            send_sem=send_c.at[number], recv_sem=recv_c.at[number],
            device_id=(ix + offset[0], iy + offset[1], iz + offset[2]), device_id_type=MESH)

    def publish(phase, block):
        project_out[phase] = block
        projects[phase, OWN * nz + iz] = block

    def project():
        both = jnp.dot(modes_t[...], halves(residual[...]), preferred_element_type=F32)
        return (both[:, :LANES] + both[:, LANES:])[:SUB]

    fetch[0].wait()
    order_rows = jnp.broadcast_to(order_ref[...].astype(F32), (LANES, m))
    order_cols = order_rows.T
    lane = lax.broadcasted_iota(jnp.int32, (m, LANES), 1).astype(F32)
    for part in range(m // LANES):
        hit = order_cols == lane + float(part * LANES)
        perm[:, part * LANES:(part + 1) * LANES] = jnp.where(hit, 1.0, 0.0).astype(BF16)

    fetch[1].wait()
    fetch[2].wait()
    mode_pad[...] = jnp.zeros_like(mode_pad)
    mode_pad[pl.ds(0, nmode)] = modes_ref[...].astype(F32)
    repeated = jnp.concatenate([mode_pad[...]] * (LANES // SUB), axis=0).T.astype(BF16)
    rows = jnp.concatenate([load_ref[...], repeated], axis=1)
    both = jnp.dot(perm[...], rows, preferred_element_type=F32)
    image[...] = both[:, :LANES]
    own_modes[...] = both[:, LANES:]

    fetch[3].wait()
    inverses[OWN] = jnp.zeros((csize, cwide), F32)
    inverses[OWN, :, pl.ds(0, csize)] = inverse_ref[...]
    publish(0, jnp.full((SUB, LANES), count_ref[0], jnp.int32).astype(F32))

    lines_x = 1 + jnp.where(ix > 0, 1, 0) + jnp.where(ix < nx - 1, 1, 0)
    lines_y = 1 + jnp.where(iy > 0, 1, 0) + jnp.where(iy < ny - 1, 1, 0)
    pl.semaphore_wait(barrier, lines_x * lines_y * nz - 1)

    every = range(len(SLOTS))
    send_slots(image, received.at[0], send_a, recv_a.at[0], every)
    send_blocks(0)
    for index, line in enumerate(LINES):
        if index != OWN:
            @pl.when(line_exists(line))
            def _(index=index):
                inverse_copy(index).start()
    send_slots(own_modes, far_modes, send_m, recv_m, every)

    for number, (offset, begin, width) in enumerate(SLOTS):
        @pl.when(jnp.logical_not(slot_exists(offset)))
        def _(number=number, begin=begin, width=width):
            arrived[number] = jnp.zeros((SUB, LANES), F32)
            received[:, pl.ds(begin, width)] = jnp.zeros((2, width, LANES), F32)
            far_modes[pl.ds(begin, width)] = jnp.zeros((width, LANES), F32)
    for index, line in enumerate(LINES):
        @pl.when(jnp.logical_not(line_exists(line)))
        def _(index=index):
            projects[:, pl.ds(index * nz, nz)] = jnp.zeros((ITERS + 1, nz, SUB, LANES), F32)
            inverses[index] = jnp.zeros((csize, cwide), F32)

    modes_t[...] = own_modes[...].T[:modes_t.shape[0]].astype(BF16)
    tile = 2 * LANES
    order_row = order_ref[...]

    def transpose_tile(step, carry):
        base = pl.multiple_of(step * tile, tile)
        row = lax.broadcasted_iota(jnp.int32, (tile, m), 0) + base
        perm_t[pl.ds(base, tile)] = jnp.where(row == order_row, 1.0, 0.0).astype(BF16)
        return carry
    lax.fori_loop(0, m // tile, transpose_tile, 0)

    fetch[4].wait()

    def first_product(step, carry):
        base = pl.multiple_of(step * tile, tile)
        half_packed[pl.ds(base, tile)] = jnp.dot(
            dual_ref[pl.ds(base, tile)], perm_t[...], preferred_element_type=F32).astype(BF16)
        return carry
    lax.fori_loop(0, m // tile, first_product, 0)

    wait_slots(image, received.at[0], send_a, recv_a.at[0])
    residual[...] = image[...] + received[0]
    wait_blocks(0)
    line_project[...] = project()
    publish(1, line_project[...])
    send_blocks(1)

    def second_product(step, carry):
        base = pl.multiple_of(step * tile, tile)
        packed[pl.ds(base, tile)] = jnp.dot(
            perm[pl.ds(base, tile)], half_packed[...], preferred_element_type=F32).astype(BF16)
        return carry
    lax.fori_loop(0, m // tile, second_product, 0)

    select_pad[...] = jnp.zeros_like(select_pad)
    sub_index = lax.broadcasted_iota(jnp.int32, (SUB, cwide), 0).astype(F32)
    position = lax.broadcasted_iota(jnp.int32, (SUB, cwide), 1).astype(F32)
    for index in range(len(LINES)):
        start = jnp.zeros((SUB, cwide), F32)
        for t in range(nz):
            count = jnp.concatenate([projects[0, index * nz + t]] * (cwide // LANES), axis=1)
            hit = (position == start + sub_index) & (sub_index < count)
            chosen = jnp.where(hit, 1.0, 0.0)
            select_pad[index, pl.ds((t + 1) * SUB, SUB)] = chosen
            select_all[pl.ds((index * nz + t) * SUB, SUB)] = chosen
            start = start + count
    for index, line in enumerate(LINES):
        if index != OWN:
            @pl.when(line_exists(line))
            def _(index=index):
                inverse_copy(8 - index).wait_recv()
                inverse_copy(index).wait_send()
    total = coarse.shape[0] // 2
    lefts = []
    for index in range(len(LINES)):
        near = select_pad[index, pl.ds(pl.multiple_of(iz * SUB, SUB), 3 * SUB)]
        both = jnp.dot(near[:, :csize].astype(BF16), halves(inverses[index]), preferred_element_type=F32)
        lefts.append(both)
    lefts.append(jnp.zeros((total - BLOCKS * SUB, 2 * cwide), F32))
    lefts = jnp.concatenate(lefts, axis=0).astype(BF16)
    whole = jnp.zeros((total, len(LINES) * line_rows), F32)
    for part in range(2):
        whole = whole + lax.dot_general(
            lefts[:, part * cwide:(part + 1) * cwide], select_all[...].astype(BF16),
            (((1,), (1,)), ((), ())), preferred_element_type=F32)
    row_line = lax.broadcasted_iota(jnp.int32, whole.shape, 0) // (3 * SUB)
    lane_line = lax.broadcasted_iota(jnp.int32, whole.shape, 1) // line_rows
    whole = jnp.where(row_line == lane_line, whole, 0.0)
    high = whole.astype(BF16)
    coarse[pl.ds(0, total)] = high
    coarse[pl.ds(total, total)] = (whole - high.astype(F32)).astype(BF16)

    wait_slots(own_modes, far_modes, send_m, recv_m)
    row_block = jnp.concatenate(
        [jnp.full((SLOTS[k][2], LANES), numbers[k], jnp.int32) for k in every], axis=0)
    lane_row = lax.broadcasted_iota(jnp.int32, (m, LANES), 1)
    for part in range(total // LANES):
        block = (lane_row + part * LANES) // SUB
        value = jnp.where(block == row_block, far_modes[...],
                          jnp.where(block == BLOCKS // 2, own_modes[...], 0.0))
        wide[:, part * LANES:(part + 1) * LANES] = value.astype(BF16)
        wide_t[part * LANES:(part + 1) * LANES] = value.T.astype(BF16)

    direction[...] = jnp.zeros_like(direction)
    multipliers[...] = jnp.zeros_like(multipliers)
    pairs = coefficients()

    def iteration(step, carry):
        keep, gain = jnp.float32(pairs[0][0]), jnp.float32(pairs[0][1])
        for k in range(1, ITERS):
            keep = jnp.where(step == k, jnp.float32(pairs[k][0]), keep)
            gain = jnp.where(step == k, jnp.float32(pairs[k][1]), gain)
        wait_blocks(step + 1)
        line_projects = projects[step + 1].reshape(len(LINES) * line_rows, LANES)
        four = jnp.dot(coarse[...], halves(line_projects), preferred_element_type=F32)
        amplitude = four[:total, :LANES] + (four[:total, LANES:] + four[total:, :LANES])
        both = jnp.dot(wide[...], halves(amplitude), preferred_element_type=F32)
        corrected = residual[...] - (both[:, :LANES] + both[:, LANES:])
        now = keep * direction[...] + gain * corrected
        direction[...] = now
        multipliers[...] = multipliers[...] + now
        rounded = now.astype(BF16)
        image[...] = jnp.dot(packed[...], rounded, preferred_element_type=F32)
        parity = lax.rem(step + 1, 2)

        @pl.when(step < ITERS - 1)
        def _():
            both = jnp.dot(wide_t[...], halves(image[...]), preferred_element_type=F32)
            shares[...] = (both[:, :LANES] + both[:, LANES:]).reshape(total // SUB, SUB, LANES)
            for number in every:
                @pl.when(slot_exists(SLOTS[number][0]))
                def _(number=number):
                    share_copy(number).start()
        send_slots(image, received.at[parity], send_a, recv_a.at[parity], every)

        @pl.when(step < ITERS - 1)
        def _():
            for number in every:
                @pl.when(slot_exists(SLOTS[number][0]))
                def _(number=number):
                    share_arrival(number).wait_recv()
                    share_copy(number).wait_send()
            terms = [shares[BLOCKS // 2]] + [arrived[number] for number in every]
            while len(terms) > 1:
                terms = [terms[k] + terms[k + 1] if k + 1 < len(terms) else terms[k]
                         for k in range(0, len(terms), 2)]
            line_project[...] = line_project[...] - terms[0]
            publish(step + 2, line_project[...])
            send_blocks(step + 2)

        @pl.when(step == ITERS - 1)
        def _():
            pair = jnp.dot(perm_t[...], halves(multipliers[...]), preferred_element_type=F32)
            mult_out[...] = pair[:, :LANES] + pair[:, LANES:]
            results[0].start()

        wait_slots(image, received.at[parity], send_a, recv_a.at[parity])
        residual[...] = residual[...] - image[...] - received[parity]
        return carry
    lax.fori_loop(0, ITERS, iteration, 0)

    pair = jnp.dot(perm_t[...], halves(residual[...]), preferred_element_type=F32)
    res_out[...] = pair[:, :LANES] + pair[:, LANES:]
    results[1].start()
    results[0].wait()
    results[1].wait()


def write_out(mult_ref, res_ref, mult_hbm, res_hbm, mult_held, res_held, read, written):
    inward = [pltpu.make_async_copy(mult_ref, mult_held, read.at[0]),
              pltpu.make_async_copy(res_ref, res_held, read.at[1])]
    outward = [pltpu.make_async_copy(mult_held, mult_hbm, written.at[0]),
               pltpu.make_async_copy(res_held, res_hbm, written.at[1])]
    for copy in inward:
        copy.start()
    for first, second in zip(inward, outward):
        first.wait()
        second.start()
    for copy in outward:
        copy.wait()


def local(shape, dual_blocks, load_terms, row_order, mode_rows, mode_count, coarse_inverse):
    nz = shape[2]
    m, loads = load_terms.shape[3:]
    csize = coarse_inverse.shape[2]
    cwide = -(-csize // LANES) * LANES
    lines = len(LINES)
    line_rows = nz * SUB
    total = -(-BLOCKS * SUB // LANES) * LANES
    hbm = pl.BlockSpec(memory_space=pltpu.HBM)
    smem = pl.BlockSpec(memory_space=pltpu.SMEM)
    rows = pltpu.VMEM((m, loads), F32)
    square = pltpu.VMEM((m, m), BF16)
    dma = pltpu.SemaphoreType.DMA
    slots = len(SLOTS)
    out = jax.ShapeDtypeStruct((m, loads), F32)
    multipliers, residual = pl.pallas_call(
        functools.partial(kernel, shape),
        out_shape=(out, out),
        in_specs=[hbm, hbm, hbm, hbm, smem, hbm],
        out_specs=(hbm, hbm),
        scratch_shapes=[
            rows, rows, dma((2,)), square, pltpu.VMEM((m, loads), BF16), pltpu.VMEM((1, m), jnp.int32),
            pltpu.VMEM((mode_rows.shape[4], m), BF16), pltpu.VMEM((csize, csize), F32), dma((5,)),
            square, square, square, square, rows, pltpu.VMEM((2, m, loads), F32), rows, rows,
            pltpu.VMEM((m, total), BF16),
            pltpu.VMEM((total, m), BF16),
            pltpu.VMEM((total // SUB, SUB, LANES), F32),
            pltpu.VMEM((slots, SUB, LANES), F32),
            pltpu.VMEM((SUB, LANES), F32),
            rows, rows, rows,
            pltpu.VMEM((2 * SUB, m), BF16),
            pltpu.VMEM((SUB, m), F32),
            pltpu.VMEM((ITERS + 1, SUB, LANES), F32),
            pltpu.VMEM((ITERS + 1, lines * nz, SUB, LANES), F32),
            pltpu.VMEM((lines, csize, cwide), F32),
            pltpu.VMEM((lines, line_rows + 2 * SUB, cwide), F32),
            pltpu.VMEM((lines * line_rows, cwide), F32),
            pltpu.VMEM((2 * total, lines * line_rows), BF16),
            dma((slots,)), dma((2, slots)), dma((slots,)), dma((slots,)), dma((slots,)), dma((slots,)),
            dma((lines,)), dma((ITERS + 1, lines)), dma((lines,)), dma((lines,)),
        ],
        compiler_params=pltpu.CompilerParams(
            collective_id=0, has_side_effects=True, vmem_limit_bytes=VMEM_BYTES),
    )(dual_blocks[0, 0, 0], load_terms[0, 0, 0], row_order[0, 0], mode_rows[0, 0, 0].T,
      mode_count.reshape(1), coarse_inverse[0, 0])
    multipliers, residual = pl.pallas_call(
        write_out,
        out_shape=(out, out),
        in_specs=[hbm, hbm],
        out_specs=(hbm, hbm),
        scratch_shapes=[rows, rows, dma((2,)), dma((2,))],
        compiler_params=pltpu.CompilerParams(vmem_limit_bytes=VMEM_BYTES),
    )(multipliers, residual)
    return multipliers[None, None, None], residual[None, None, None]


def solution(mesh):
    shape = tuple(mesh.shape[name] for name in ("gx", "gy", "gz"))
    in_specs = (
        P("gx", "gy", "gz", None, None),
        P("gx", "gy", "gz", None, None),
        P("gx", "gy", "gz", None),
        P("gx", "gy", "gz", None, None),
        P("gx", "gy", "gz"),
        P("gx", "gy", None, None),
    )
    out_specs = (P("gx", "gy", "gz", None, None), P("gx", "gy", "gz", None, None))
    return jax.shard_map(functools.partial(local, shape), mesh=mesh, in_specs=in_specs,
                         out_specs=out_specs, check_vma=False)
```

```python
import functools

import jax
import jax.numpy as jnp
from jax import lax
from jax.experimental import pallas as pl
from jax.experimental.pallas import tpu as pltpu
from jax.sharding import PartitionSpec as P

FACE = 128
EDGE = 16
CORNER = 8
ITERS = 3
EIG_LOW = 0.5
EIG_HIGH = 6.0

MESH = pl.DeviceIdType.MESH
LANES = 128
VMEM_BYTES = 62 * 1024 * 1024
PIECES = 4
SUB = 8
F32 = jnp.float32
BF16 = jnp.bfloat16


def slot_table():
    slots = []
    begin = 0
    for weight, width in ((1, FACE), (2, EDGE), (3, CORNER)):
        for a in (-1, 0, 1):
            for b in (-1, 0, 1):
                for c in (-1, 0, 1):
                    if abs(a) + abs(b) + abs(c) == weight:
                        slots.append(((a, b, c), begin, width))
                        begin += width
    return slots


SLOTS = slot_table()
BEGIN = {offset: begin for offset, begin, _ in SLOTS}
LINES = [(a, b) for a in (-1, 0, 1) for b in (-1, 0, 1)]
OWN = 4
BLOCKS = 3 * len(LINES)


def coefficients():
    center = 0.5 * (EIG_HIGH + EIG_LOW)
    half = 0.5 * (EIG_HIGH - EIG_LOW)
    pairs = [(0.0, 1.0 / center)]
    rho = half / center
    for _ in range(1, ITERS):
        following = 1.0 / (2.0 * center / half - rho)
        pairs.append((following * rho, 2.0 * following / half))
        rho = following
    return pairs


def halves(x):
    high = x.astype(BF16)
    low = (x - high.astype(F32)).astype(BF16)
    return jnp.concatenate([high, low], axis=1)


def kernel(shape, dual_hbm, load_hbm, order_hbm, modes_hbm, count_ref, inverse_hbm,
           mult_hbm, res_hbm,
           mult_out, res_out, written, dual_ref, load_ref, order_ref, modes_ref, inverse_ref, fetched,
           perm, perm_t, half_packed, packed, image, received, own_modes, far_modes, wide,
           wide_t, shares, arrived, line_project,
           residual, direction, multipliers, modes_t, mode_pad,
           project_out, projects, inverses, select_pad, select_all, coarse,
           send_a, recv_a, send_m, recv_m, send_c, recv_c, send_b, recv_b, send_i, recv_i):
    nx, ny, nz = shape
    ix, iy, iz = lax.axis_index("gx"), lax.axis_index("gy"), lax.axis_index("gz")
    numbers = [(((o[0] + 1) * 3 + o[1] + 1) * 3 + o[2] + 1) for o, _, _ in SLOTS]
    nmode = modes_ref.shape[0]
    csize = inverse_ref.shape[0]
    cwide = inverses.shape[2]
    line_rows = nz * SUB
    fetch = [pltpu.make_async_copy(source, target, fetched.at[k]) for k, (source, target) in enumerate(
        ((order_hbm, order_ref), (load_hbm, load_ref), (modes_hbm, modes_ref),
         (inverse_hbm, inverse_ref), (dual_hbm, dual_ref)))]
    for copy in fetch:
        copy.start()
    m = dual_ref.shape[0]
    cut = m // 2
    results = [pltpu.make_async_copy(mult_out, mult_hbm, written.at[0])] + [
        pltpu.make_async_copy(res_out.at[pl.ds(k * cut, cut)], res_hbm.at[pl.ds(k * cut, cut)], written.at[1 + k])
        for k in range(2)]
    barrier = pltpu.get_barrier_semaphore()

    def line_exists(line):
        a, b = line
        return (ix + a >= 0) & (ix + a < nx) & (iy + b >= 0) & (iy + b < ny)

    def slot_exists(offset):
        return line_exists(offset[:2]) & (iz + offset[2] >= 0) & (iz + offset[2] < nz)

    def each_device(line_index, action):
        def step(t, carry):
            if line_index == OWN:
                @pl.when(t != iz)
                def _():
                    action(t)
            else:
                action(t)
            return carry
        lax.fori_loop(0, nz, step, 0, unroll=nz <= 4)

    for index, line in enumerate(LINES):
        @pl.when(line_exists(line))
        def _(index=index, line=line):
            def greet(t):
                pl.semaphore_signal(barrier, inc=1, device_id=(ix + line[0], iy + line[1], t),
                                    device_id_type=MESH)
            each_device(index, greet)

    def slot_copy(source, target, send, recv, number):
        offset, begin, width = SLOTS[number]
        back = (-offset[0], -offset[1], -offset[2])
        return pltpu.make_async_remote_copy(
            src_ref=source.at[pl.ds(begin, width)],
            dst_ref=target.at[pl.ds(BEGIN[back], width)],
            send_sem=send.at[number],
            recv_sem=recv.at[[s[0] for s in SLOTS].index(back)],
            device_id=(ix + offset[0], iy + offset[1], iz + offset[2]),
            device_id_type=MESH)

    def slot_arrival(target, send, recv, number):
        offset, begin, width = SLOTS[number]
        return pltpu.make_async_remote_copy(
            src_ref=target.at[pl.ds(begin, width)],
            dst_ref=target.at[pl.ds(begin, width)],
            send_sem=send.at[number], recv_sem=recv.at[number],
            device_id=(ix + offset[0], iy + offset[1], iz + offset[2]),
            device_id_type=MESH)

    def send_slots(source, target, send, recv, numbers):
        for number in numbers:
            @pl.when(slot_exists(SLOTS[number][0]))
            def _(number=number):
                slot_copy(source, target, send, recv, number).start()

    def wait_slots(source, target, send, recv):
        for number in range(len(SLOTS)):
            @pl.when(slot_exists(SLOTS[number][0]))
            def _(number=number):
                slot_arrival(target, send, recv, number).wait_recv()
                slot_copy(source, target, send, recv, number).wait_send()

    def send_blocks(phase):
        for index, line in enumerate(LINES):
            @pl.when(line_exists(line))
            def _(index=index, line=line):
                def copy(t):
                    pltpu.make_async_remote_copy(
                        src_ref=project_out.at[phase],
                        dst_ref=projects.at[phase, (8 - index) * nz + iz],
                        send_sem=send_b.at[index],
                        recv_sem=recv_b.at[phase, 8 - index],
                        device_id=(ix + line[0], iy + line[1], t),
                        device_id_type=MESH).start()
                each_device(index, copy)

    def wait_blocks(phase):
        for index, line in enumerate(LINES):
            blocks = nz - 1 if index == OWN else nz
            if blocks == 0:
                continue
            @pl.when(line_exists(line))
            def _(index=index, line=line, blocks=blocks):
                span = projects.at[phase, pl.ds(index * nz, blocks)]
                arrival = pltpu.make_async_remote_copy(
                    src_ref=span, dst_ref=span,
                    send_sem=send_b.at[index], recv_sem=recv_b.at[phase, index],
                    device_id=(ix + line[0], iy + line[1], iz), device_id_type=MESH)
                arrival.wait_recv()
                arrival.wait_send()

    def inverse_copy(index):
        line = LINES[index]
        return pltpu.make_async_remote_copy(
            src_ref=inverses.at[OWN], dst_ref=inverses.at[8 - index],
            send_sem=send_i.at[index], recv_sem=recv_i.at[8 - index],
            device_id=(ix + line[0], iy + line[1], iz), device_id_type=MESH)

    def share_copy(number):
        offset = SLOTS[number][0]
        other = [s[0] for s in SLOTS].index((-offset[0], -offset[1], -offset[2]))
        return pltpu.make_async_remote_copy(
            src_ref=shares.at[numbers[number]], dst_ref=arrived.at[other],
            send_sem=send_c.at[number], recv_sem=recv_c.at[other],
            device_id=(ix + offset[0], iy + offset[1], iz + offset[2]), device_id_type=MESH)

    def share_arrival(number):
        offset = SLOTS[number][0]
        return pltpu.make_async_remote_copy(
            src_ref=arrived.at[number], dst_ref=arrived.at[number],
            send_sem=send_c.at[number], recv_sem=recv_c.at[number],
            device_id=(ix + offset[0], iy + offset[1], iz + offset[2]), device_id_type=MESH)

    def publish(phase, block):
        project_out[phase] = block
        projects[phase, OWN * nz + iz] = block

    def project():
        both = jnp.dot(modes_t[...], halves(residual[...]), preferred_element_type=F32)
        return (both[:, :LANES] + both[:, LANES:])[:SUB]

    fetch[0].wait()
    order_rows = jnp.broadcast_to(order_ref[...].astype(F32), (LANES, m))
    order_cols = order_rows.T
    lane = lax.broadcasted_iota(jnp.int32, (m, LANES), 1).astype(F32)
    for part in range(m // LANES):
        hit = order_cols == lane + float(part * LANES)
        perm[:, part * LANES:(part + 1) * LANES] = jnp.where(hit, 1.0, 0.0).astype(BF16)

    fetch[1].wait()
    fetch[2].wait()
    mode_pad[...] = jnp.zeros_like(mode_pad)
    mode_pad[pl.ds(0, nmode)] = modes_ref[...].astype(F32)
    repeated = jnp.concatenate([mode_pad[...]] * (LANES // SUB), axis=0).T.astype(BF16)
    rows = jnp.concatenate([load_ref[...], repeated], axis=1)
    both = jnp.dot(perm[...], rows, preferred_element_type=F32)
    image[...] = both[:, :LANES]
    own_modes[...] = both[:, LANES:]

    fetch[3].wait()
    inverses[OWN] = jnp.zeros((csize, cwide), F32)
    inverses[OWN, :, pl.ds(0, csize)] = inverse_ref[...]
    publish(0, jnp.full((SUB, LANES), count_ref[0], jnp.int32).astype(F32))

    lines_x = 1 + jnp.where(ix > 0, 1, 0) + jnp.where(ix < nx - 1, 1, 0)
    lines_y = 1 + jnp.where(iy > 0, 1, 0) + jnp.where(iy < ny - 1, 1, 0)
    pl.semaphore_wait(barrier, lines_x * lines_y * nz - 1)

    every = range(len(SLOTS))
    send_slots(image, received.at[0], send_a, recv_a.at[0], every)
    send_blocks(0)
    for index, line in enumerate(LINES):
        if index != OWN:
            @pl.when(line_exists(line))
            def _(index=index):
                inverse_copy(index).start()

    for number, (offset, begin, width) in enumerate(SLOTS):
        @pl.when(jnp.logical_not(slot_exists(offset)))
        def _(number=number, begin=begin, width=width):
            arrived[number] = jnp.zeros((SUB, LANES), F32)
            received[:, pl.ds(begin, width)] = jnp.zeros((2, width, LANES), F32)
            far_modes[pl.ds(begin, width)] = jnp.zeros((width, LANES), F32)
    for index, line in enumerate(LINES):
        @pl.when(jnp.logical_not(line_exists(line)))
        def _(index=index):
            projects[:, pl.ds(index * nz, nz)] = jnp.zeros((ITERS + 1, nz, SUB, LANES), F32)
            inverses[index] = jnp.zeros((csize, cwide), F32)

    modes_t[...] = own_modes[...].T[:modes_t.shape[0]].astype(BF16)
    tile = 2 * LANES
    order_row = order_ref[...]

    def transpose_tile(step, carry):
        base = pl.multiple_of(step * tile, tile)
        row = lax.broadcasted_iota(jnp.int32, (tile, m), 0) + base
        perm_t[pl.ds(base, tile)] = jnp.where(row == order_row, 1.0, 0.0).astype(BF16)
        return carry
    lax.fori_loop(0, m // tile, transpose_tile, 0)

    fetch[4].wait()

    def first_product(step, carry):
        base = pl.multiple_of(step * tile, tile)
        half_packed[pl.ds(base, tile)] = jnp.dot(
            dual_ref[pl.ds(base, tile)], perm_t[...], preferred_element_type=F32).astype(BF16)
        return carry
    lax.fori_loop(0, m // tile, first_product, 0)
    send_slots(own_modes, far_modes, send_m, recv_m, every)

    wait_slots(image, received.at[0], send_a, recv_a.at[0])
    residual[...] = image[...] + received[0]
    wait_blocks(0)
    line_project[...] = project()
    publish(1, line_project[...])
    send_blocks(1)

    def second_product(step, carry):
        base = pl.multiple_of(step * tile, tile)
        packed[pl.ds(base, tile)] = jnp.dot(
            perm[pl.ds(base, tile)], half_packed[...], preferred_element_type=F32).astype(BF16)
        return carry
    lax.fori_loop(0, m // tile, second_product, 0)

    select_pad[...] = jnp.zeros_like(select_pad)
    sub_index = lax.broadcasted_iota(jnp.int32, (SUB, cwide), 0).astype(F32)
    position = lax.broadcasted_iota(jnp.int32, (SUB, cwide), 1).astype(F32)
    for index in range(len(LINES)):
        start = jnp.zeros((SUB, cwide), F32)
        for t in range(nz):
            count = jnp.concatenate([projects[0, index * nz + t]] * (cwide // LANES), axis=1)
            hit = (position == start + sub_index) & (sub_index < count)
            chosen = jnp.where(hit, 1.0, 0.0)
            select_pad[index, pl.ds((t + 1) * SUB, SUB)] = chosen
            select_all[pl.ds((index * nz + t) * SUB, SUB)] = chosen
            start = start + count
    for index, line in enumerate(LINES):
        if index != OWN:
            @pl.when(line_exists(line))
            def _(index=index):
                inverse_copy(8 - index).wait_recv()
                inverse_copy(index).wait_send()
    total = coarse.shape[0] // 2
    lefts = []
    for index in range(len(LINES)):
        near = select_pad[index, pl.ds(pl.multiple_of(iz * SUB, SUB), 3 * SUB)]
        both = jnp.dot(near[:, :csize].astype(BF16), halves(inverses[index]), preferred_element_type=F32)
        lefts.append(both)
    lefts.append(jnp.zeros((total - BLOCKS * SUB, 2 * cwide), F32))
    lefts = jnp.concatenate(lefts, axis=0).astype(BF16)
    whole = jnp.zeros((total, len(LINES) * line_rows), F32)
    for part in range(2):
        whole = whole + lax.dot_general(
            lefts[:, part * cwide:(part + 1) * cwide], select_all[...].astype(BF16),
            (((1,), (1,)), ((), ())), preferred_element_type=F32)
    row_line = lax.broadcasted_iota(jnp.int32, whole.shape, 0) // (3 * SUB)
    lane_line = lax.broadcasted_iota(jnp.int32, whole.shape, 1) // line_rows
    whole = jnp.where(row_line == lane_line, whole, 0.0)
    high = whole.astype(BF16)
    coarse[pl.ds(0, total)] = high
    coarse[pl.ds(total, total)] = (whole - high.astype(F32)).astype(BF16)

    wait_slots(own_modes, far_modes, send_m, recv_m)
    row_block = jnp.concatenate(
        [jnp.full((SLOTS[k][2], LANES), numbers[k], jnp.int32) for k in every], axis=0)
    lane_row = lax.broadcasted_iota(jnp.int32, (m, LANES), 1)
    for part in range(total // LANES):
        block = (lane_row + part * LANES) // SUB
        value = jnp.where(block == row_block, far_modes[...],
                          jnp.where(block == BLOCKS // 2, own_modes[...], 0.0))
        wide[:, part * LANES:(part + 1) * LANES] = value.astype(BF16)
        wide_t[part * LANES:(part + 1) * LANES] = value.T.astype(BF16)

    direction[...] = jnp.zeros_like(direction)
    multipliers[...] = jnp.zeros_like(multipliers)
    pairs = coefficients()

    def iteration(step, carry):
        keep, gain = jnp.float32(pairs[0][0]), jnp.float32(pairs[0][1])
        for k in range(1, ITERS):
            keep = jnp.where(step == k, jnp.float32(pairs[k][0]), keep)
            gain = jnp.where(step == k, jnp.float32(pairs[k][1]), gain)
        wait_blocks(step + 1)
        line_projects = projects[step + 1].reshape(len(LINES) * line_rows, LANES)
        four = jnp.dot(coarse[...], halves(line_projects), preferred_element_type=F32)
        amplitude = four[:total, :LANES] + (four[:total, LANES:] + four[total:, :LANES])
        both = jnp.dot(wide[...], halves(amplitude), preferred_element_type=F32)
        corrected = residual[...] - (both[:, :LANES] + both[:, LANES:])
        now = keep * direction[...] + gain * corrected
        direction[...] = now
        multipliers[...] = multipliers[...] + now
        rounded = now.astype(BF16)
        image[...] = jnp.dot(packed[...], rounded, preferred_element_type=F32)
        parity = lax.rem(step + 1, 2)

        @pl.when(step < ITERS - 1)
        def _():
            both = jnp.dot(wide_t[...], halves(image[...]), preferred_element_type=F32)
            shares[...] = (both[:, :LANES] + both[:, LANES:]).reshape(total // SUB, SUB, LANES)
            for number in every:
                @pl.when(slot_exists(SLOTS[number][0]))
                def _(number=number):
                    share_copy(number).start()
        send_slots(image, received.at[parity], send_a, recv_a.at[parity], every)

        @pl.when(step < ITERS - 1)
        def _():
            for number in every:
                @pl.when(slot_exists(SLOTS[number][0]))
                def _(number=number):
                    share_arrival(number).wait_recv()
                    share_copy(number).wait_send()
            terms = [shares[BLOCKS // 2]] + [arrived[number] for number in every]
            while len(terms) > 1:
                terms = [terms[k] + terms[k + 1] if k + 1 < len(terms) else terms[k]
                         for k in range(0, len(terms), 2)]
            line_project[...] = line_project[...] - terms[0]
            publish(step + 2, line_project[...])
            send_blocks(step + 2)

        @pl.when(step == ITERS - 1)
        def _():
            pair = jnp.dot(perm_t[...], halves(multipliers[...]), preferred_element_type=F32)
            mult_out[...] = pair[:, :LANES] + pair[:, LANES:]
            results[0].start()

        wait_slots(image, received.at[parity], send_a, recv_a.at[parity])
        residual[...] = residual[...] - image[...] - received[parity]
        return carry
    lax.fori_loop(0, ITERS, iteration, 0)

    parts = halves(residual[...])
    for k in range(2):
        pair = jnp.dot(perm_t[pl.ds(k * cut, cut)], parts, preferred_element_type=F32)
        res_out[pl.ds(k * cut, cut)] = pair[:, :LANES] + pair[:, LANES:]
        results[1 + k].start()
    for copy in results:
        copy.wait()


def write_out(mult_ref, res_ref, mult_hbm, res_hbm, mult_held, res_held, read, written):
    rows = mult_ref.shape[0] // PIECES
    inward, outward = [], []
    for piece in range(PIECES):
        span = pl.ds(piece * rows, rows)
        for k, (source, held, target) in enumerate(((mult_ref, mult_held, mult_hbm), (res_ref, res_held, res_hbm))):
            inward.append(pltpu.make_async_copy(source.at[span], held.at[span], read.at[k, piece]))
            outward.append(pltpu.make_async_copy(held.at[span], target.at[span], written.at[k, piece]))
    for copy in inward:
        copy.start()
    for first, second in zip(inward, outward):
        first.wait()
        second.start()
    for copy in outward:
        copy.wait()


def local(shape, dual_blocks, load_terms, row_order, mode_rows, mode_count, coarse_inverse):
    nz = shape[2]
    m, loads = load_terms.shape[3:]
    csize = coarse_inverse.shape[2]
    cwide = -(-csize // LANES) * LANES
    lines = len(LINES)
    line_rows = nz * SUB
    total = -(-BLOCKS * SUB // LANES) * LANES
    hbm = pl.BlockSpec(memory_space=pltpu.HBM)
    smem = pl.BlockSpec(memory_space=pltpu.SMEM)
    rows = pltpu.VMEM((m, loads), F32)
    square = pltpu.VMEM((m, m), BF16)
    dma = pltpu.SemaphoreType.DMA
    slots = len(SLOTS)
    out = jax.ShapeDtypeStruct((m, loads), F32)
    multipliers, residual = pl.pallas_call(
        functools.partial(kernel, shape),
        out_shape=(out, out),
        in_specs=[hbm, hbm, hbm, hbm, smem, hbm],
        out_specs=(hbm, hbm),
        scratch_shapes=[
            rows, rows, dma((3,)), square, pltpu.VMEM((m, loads), BF16), pltpu.VMEM((1, m), jnp.int32),
            pltpu.VMEM((mode_rows.shape[4], m), BF16), pltpu.VMEM((csize, csize), F32), dma((5,)),
            square, square, square, square, rows, pltpu.VMEM((2, m, loads), F32), rows, rows,
            pltpu.VMEM((m, total), BF16),
            pltpu.VMEM((total, m), BF16),
            pltpu.VMEM((total // SUB, SUB, LANES), F32),
            pltpu.VMEM((slots, SUB, LANES), F32),
            pltpu.VMEM((SUB, LANES), F32),
            rows, rows, rows,
            pltpu.VMEM((2 * SUB, m), BF16),
            pltpu.VMEM((SUB, m), F32),
            pltpu.VMEM((ITERS + 1, SUB, LANES), F32),
            pltpu.VMEM((ITERS + 1, lines * nz, SUB, LANES), F32),
            pltpu.VMEM((lines, csize, cwide), F32),
            pltpu.VMEM((lines, line_rows + 2 * SUB, cwide), F32),
            pltpu.VMEM((lines * line_rows, cwide), F32),
            pltpu.VMEM((2 * total, lines * line_rows), BF16),
            dma((slots,)), dma((2, slots)), dma((slots,)), dma((slots,)), dma((slots,)), dma((slots,)),
            dma((lines,)), dma((ITERS + 1, lines)), dma((lines,)), dma((lines,)),
        ],
        compiler_params=pltpu.CompilerParams(
            collective_id=0, has_side_effects=True, vmem_limit_bytes=VMEM_BYTES),
    )(dual_blocks[0, 0, 0], load_terms[0, 0, 0], row_order[0, 0], mode_rows[0, 0, 0].T,
      mode_count.reshape(1), coarse_inverse[0, 0])
    multipliers, residual = pl.pallas_call(
        write_out,
        out_shape=(out, out),
        in_specs=[hbm, hbm],
        out_specs=(hbm, hbm),
        scratch_shapes=[rows, rows, dma((2, PIECES)), dma((2, PIECES))],
        compiler_params=pltpu.CompilerParams(vmem_limit_bytes=VMEM_BYTES),
    )(multipliers, residual)
    return multipliers[None, None, None], residual[None, None, None]


def solution(mesh):
    shape = tuple(mesh.shape[name] for name in ("gx", "gy", "gz"))
    in_specs = (
        P("gx", "gy", "gz", None, None),
        P("gx", "gy", "gz", None, None),
        P("gx", "gy", "gz", None),
        P("gx", "gy", "gz", None, None),
        P("gx", "gy", "gz"),
        P("gx", "gy", None, None),
    )
    out_specs = (P("gx", "gy", "gz", None, None), P("gx", "gy", "gz", None, None))
    return jax.shard_map(functools.partial(local, shape), mesh=mesh, in_specs=in_specs,
                         out_specs=out_specs, check_vma=False)
```
